512 devices in a mesh: dof: 16 (over y, z_hi), atom: 32 (over x, z_lo, core).
Axes of the slice: x: 4, y: 4, z: 16 (z_hi: 4, z_lo: 4; z = z_hi * 4 + z_lo), core: 2. Of those that a mesh axis runs over, the one named last changes fastest.
Arguments:
- received: bfloat16 [2, 64, 8192], P(None, None, 'dof'), may hold values from -6 to 6
- codes_now: bfloat16 [2, 64, 65536], P(None, 'dof', 'atom'), may hold values from -6 to 6
- ridge_tiles: bfloat16 [16, 32, 4, 2, 128, 128], P('dof', 'atom'), may hold values from -0.0625 to 0.0625
- coords: int32 [16, 32, 4, 2], P('dof', 'atom'), may hold values from 0 to 15, as said below
- tile_counts: int32 [16, 32], P('dof', 'atom'), may hold values from 1 to 4, as said below
- group_ids: int32 [512], P('atom'), may hold values from 0 to 7
- thresholds: float32 [8], replicated, may hold values from 0.1 to 1
- cotangent: bfloat16 [2, 64, 65536], P(None, 'dof', 'atom'), may hold values from -6 to 6
Outputs:
- codes_next: bfloat16 [2, 64, 65536], P(None, 'dof', 'atom')
- tile_grads: bfloat16 [16, 32, 4, 2, 128, 128], P('dof', 'atom')
- threshold_grads: float32 [8], replicated
The draws below stay inside these ranges and needn't reach their ends.
Inputs may be any that keep to these rules, and one draw needn't show every extreme that they name: coords[p, q, l] = (row tile under 0 to 3, atom tile under 0 to 15) of device (p, q); row tiles follow the atom tiles along a ridge; a pair may repeat. Slots l >= tile_counts of a device are empty; some device has all 4 live.
All inputs are finite; a program needn't handle non-finite values.
Results may differ from the reference program's by a relative error of at most 0.03565.
The reference program's roundings to bfloat16 on the way count: a program that leaves them out, or rounds other values in their place, can miss the bound.
Values may be sent and summed in bfloat16 or wider, within the bound.
A program may use at most 192 MiB of HBM per device.

```python
import math
import jax
import jax.numpy as jnp
from jax import lax

TILE = 128
M = 8192
NATOM = 65536
SNAP = 64
SLOTS = 4
GROUPS = 8
RT_DEV = 4
CT_DEV = 16
ATOM_BLOCKS = 512
N_DOF = 16
N_ATOM = 32


def draw_coords(key, part):
    key = jax.random.fold_in(key, 11)
    first, second = jax.random.split(key)
    atom_tile = jax.random.randint(first, (N_DOF, N_ATOM, SLOTS), 0, CT_DEV)
    jitter = jax.random.randint(second, (N_DOF, N_ATOM, SLOTS), 0, 2)
    row_tile = (atom_tile * RT_DEV // CT_DEV + jitter) % RT_DEV
    return jnp.stack([row_tile, atom_tile], axis=-1).astype(jnp.int32)


def draw_tile_counts(key, part):
    key = jax.random.fold_in(key, 23)
    first, second = jax.random.split(key)
    base = jax.random.randint(first, (N_DOF * N_ATOM,), 1, SLOTS + 1)
    chosen = jax.random.randint(second, (), 0, N_DOF * N_ATOM)
    flat = jnp.where(jnp.arange(N_DOF * N_ATOM) == chosen, SLOTS, base)
    return flat.reshape(N_DOF, N_ATOM).astype(jnp.int32)


def set_ends(values, rng, low, top_value):
    longest = values.shape.index(max(values.shape))
    spots = []
    for shift in (0, 1):
        where = [jax.random.randint(jax.random.fold_in(rng, axis), (), 0, length) for axis, length in enumerate(values.shape)]
        where[longest] = (where[longest] + shift) % values.shape[longest]
        spots.append(tuple(where))
    return values.at[spots[0]].set(low).at[spots[1]].set(top_value)


def steps_of(stream_key, dims, shards, smallest, top_value):
    def one(position, blocks):
        steps = jax.random.uniform(jax.random.fold_in(jax.random.fold_in(stream_key, 6), position), (blocks,), jnp.float32, smallest / len(shards), top_value / len(shards))
        return jnp.repeat(jnp.exp(steps), dims[position] // blocks).reshape((-1,) + (1,) * (len(dims) - position - 1))

    factor_of = one(*shards[0])
    for cut in shards[1:]:
        factor_of = factor_of * one(*cut)
    return factor_of


def noise(own_key, extent, scale, most, cuts=(), held_as=jnp.bfloat16):
    loudness = steps_of(own_key, extent, cuts, -0.22, 0.18) if cuts else 1.0
    values = jax.random.normal(own_key, extent, jnp.float32) * scale * loudness
    return jnp.minimum(jnp.maximum(values, -most), most).astype(held_as)


def setup_inputs(seed: int = 0) -> dict:
    key_of = jax.random.split(jax.random.key(seed), 9)
    received = noise(key_of[0], (2, SNAP, M), 1.0, 6.0, ((2, 16),))
    codes_now = noise(key_of[1], (2, SNAP, NATOM), 1.0, 6.0, ((1, 16), (2, 32)))
    ridge_tiles = noise(key_of[2], (N_DOF, N_ATOM, SLOTS, 2, TILE, TILE), (2 * TILE * SLOTS * N_ATOM // RT_DEV) ** -0.5, 0.0625, ((0, 16), (1, 32)))
    coords = draw_coords(jax.random.fold_in(key_of[8], 71), 0)
    tile_counts = draw_tile_counts(jax.random.fold_in(key_of[8], 71), 0)
    group_ids = set_ends(jax.random.randint(key_of[5], (ATOM_BLOCKS,), 0, GROUPS), jax.random.fold_in(key_of[5], 1), 0, GROUPS - 1).astype(jnp.int32)
    thresholds = jnp.clip(jnp.exp(jax.random.uniform(key_of[6], (GROUPS,), jnp.float32, math.log(0.1), math.log(1.0))), 0.1, 1.0)
    cotangent = noise(key_of[7], (2, SNAP, NATOM), 1.0, 6.0, ((1, 16), (2, 32)))
    return dict(received=received, codes_now=codes_now, ridge_tiles=ridge_tiles, coords=coords, tile_counts=tile_counts, group_ids=group_ids, thresholds=thresholds, cotangent=cotangent)


def shrink(field, theta_atom):
    magnitude = jnp.sqrt(field[0] * field[0] + field[1] * field[1] + 1e-06)
    factor = jnp.maximum(magnitude - theta_atom, 0.0) / jnp.maximum(magnitude, theta_atom)
    return field * factor

def ridge_apply(tiles_live, codes_block, col_index, rows_hot):
    halves, snapshots, columns = codes_block.shape
    tile_size = tiles_live.shape[-1]
    blocks = codes_block.reshape(halves, snapshots, columns // tile_size, tile_size)
    picked = jnp.take(blocks, col_index, axis=2)
    product = jnp.einsum('lcab,dslb->cdsla', tiles_live.astype(jnp.float32), picked.astype(jnp.float32))
    stacked = jnp.stack([product[0, 0] - product[1, 1], product[0, 1] + product[1, 0]])
    placed = jnp.einsum('esla,lr->esra', stacked, rows_hot, precision=lax.Precision.HIGHEST)
    return placed.reshape(halves, snapshots, -1)

def ridge_adjoint(tiles_live, resid_block, row_index, cols_hot):
    halves, snapshots, rows_width = resid_block.shape
    tile_size = tiles_live.shape[-1]
    blocks = resid_block.reshape(halves, snapshots, rows_width // tile_size, tile_size)
    picked = jnp.take(blocks, row_index, axis=2)
    product = jnp.einsum('lcab,dsla->cdslb', tiles_live.astype(jnp.float32), picked.astype(jnp.float32))
    stacked = jnp.stack([product[0, 0] + product[1, 1], product[0, 1] - product[1, 0]])
    placed = jnp.einsum('eslb,lk->eskb', stacked, cols_hot, precision=lax.Precision.HIGHEST)
    return placed.reshape(halves, snapshots, -1)

def ridge_grads(resid_block, grad_codes, grad_resid, codes_block, row_index, col_index, tile_size):
    halves, snapshots, rows_width = resid_block.shape
    atoms_width = codes_block.shape[2]

    def pick(array, width, index):
        return jnp.take(array.reshape(halves, snapshots, width // tile_size, tile_size), index, axis=2).astype(jnp.float32)
    left = jnp.einsum('csla,dslb->cdlab', pick(resid_block, rows_width, row_index), pick(grad_codes, atoms_width, col_index))
    right = jnp.einsum('csla,dslb->cdlab', pick(grad_resid, rows_width, row_index), pick(codes_block, atoms_width, col_index))
    grad_real = left[0, 0] + left[1, 1] - right[0, 0] - right[1, 1]
    grad_imag = left[1, 0] - left[0, 1] + right[0, 1] - right[1, 0]
    return jnp.stack([grad_real, grad_imag], axis=1)

def device_parts(ridge_tiles, coords, tile_counts, device):
    dof_index = device // N_ATOM
    atom_index = device % N_ATOM
    tile_set = ridge_tiles[dof_index, atom_index]
    coord_set = coords[dof_index, atom_index]
    live = (jnp.arange(SLOTS).astype(jnp.int32) < tile_counts[dof_index, atom_index]).astype(jnp.float32)
    tiles_live = tile_set * live.astype(jnp.bfloat16)[:, None, None, None]
    rows_hot = (coord_set[:, 0][:, None] == jnp.arange(RT_DEV).astype(jnp.int32)[None, :]).astype(jnp.float32)
    cols_hot = (coord_set[:, 1][:, None] == jnp.arange(CT_DEV).astype(jnp.int32)[None, :]).astype(jnp.float32)
    return (dof_index, atom_index, tiles_live, coord_set, rows_hot, cols_hot, live)

def reference(received, codes_now, ridge_tiles, coords, tile_counts, group_ids, thresholds, cotangent):
    rows_dev = RT_DEV * TILE
    atoms_dev = CT_DEV * TILE
    total = N_DOF * N_ATOM

    def fit_step(device, accum):
        dof_index, atom_index, tiles_live, coord_set, rows_hot, cols_hot, live = device_parts(ridge_tiles, coords, tile_counts, device)
        block = lax.dynamic_slice_in_dim(codes_now, (atom_index * atoms_dev).astype(jnp.int32), atoms_dev, 2)
        part = ridge_apply(tiles_live, block, coord_set[:, 1], rows_hot)
        start = (dof_index * rows_dev).astype(jnp.int32)
        current = lax.dynamic_slice_in_dim(accum, start, rows_dev, 2)
        return lax.dynamic_update_slice_in_dim(accum, current + part, start, 2)
    fitted = lax.fori_loop(0, total, fit_step, jnp.zeros((2, SNAP, M), jnp.float32))
    residual = (received.astype(jnp.float32) - fitted).astype(jnp.bfloat16)

    def corr_step(device, accum):
        dof_index, atom_index, tiles_live, coord_set, rows_hot, cols_hot, live = device_parts(ridge_tiles, coords, tile_counts, device)
        block = lax.dynamic_slice_in_dim(residual, (dof_index * rows_dev).astype(jnp.int32), rows_dev, 2)
        part = ridge_adjoint(tiles_live, block, coord_set[:, 0], cols_hot)
        start = (atom_index * atoms_dev).astype(jnp.int32)
        current = lax.dynamic_slice_in_dim(accum, start, atoms_dev, 2)
        return lax.dynamic_update_slice_in_dim(accum, current + part, start, 2)
    correlation = lax.fori_loop(0, total, corr_step, jnp.zeros((2, SNAP, NATOM), jnp.float32))
    field = codes_now.astype(jnp.float32) + correlation
    group_atoms = jnp.repeat(group_ids, TILE)
    onehot = (group_atoms[:, None] == jnp.arange(GROUPS).astype(jnp.int32)[None, :]).astype(jnp.float32)
    theta_atom = jnp.dot(onehot, thresholds, precision=lax.Precision.HIGHEST)
    shrunk, pull = jax.vjp(shrink, field, theta_atom)
    grad_field, grad_theta = pull(cotangent.astype(jnp.float32))
    codes_next = shrunk.astype(jnp.bfloat16)
    grad_codes = grad_field.astype(jnp.bfloat16)
    threshold_grads = jnp.dot(grad_theta, onehot, precision=lax.Precision.HIGHEST)

    def back_step(device, accum):
        dof_index, atom_index, tiles_live, coord_set, rows_hot, cols_hot, live = device_parts(ridge_tiles, coords, tile_counts, device)
        block = lax.dynamic_slice_in_dim(grad_codes, (atom_index * atoms_dev).astype(jnp.int32), atoms_dev, 2)
        part = ridge_apply(tiles_live, block, coord_set[:, 1], rows_hot)
        start = (dof_index * rows_dev).astype(jnp.int32)
        current = lax.dynamic_slice_in_dim(accum, start, rows_dev, 2)
        return lax.dynamic_update_slice_in_dim(accum, current + part, start, 2)
    grad_resid = lax.fori_loop(0, total, back_step, jnp.zeros((2, SNAP, M), jnp.float32)).astype(jnp.bfloat16)

    def grad_device(device):
        dof_index, atom_index, tiles_live, coord_set, rows_hot, cols_hot, live = device_parts(ridge_tiles, coords, tile_counts, device)
        row_start = (dof_index * rows_dev).astype(jnp.int32)
        atom_start = (atom_index * atoms_dev).astype(jnp.int32)
        grads = ridge_grads(lax.dynamic_slice_in_dim(residual, row_start, rows_dev, 2), lax.dynamic_slice_in_dim(grad_codes, atom_start, atoms_dev, 2), lax.dynamic_slice_in_dim(grad_resid, row_start, rows_dev, 2), lax.dynamic_slice_in_dim(codes_now, atom_start, atoms_dev, 2), coord_set[:, 0], coord_set[:, 1], TILE)
        return (grads * live[:, None, None, None]).astype(jnp.bfloat16)
    tile_grads = lax.map(grad_device, jnp.arange(total).astype(jnp.int32))
    tile_grads = tile_grads.reshape(N_DOF, N_ATOM, SLOTS, 2, TILE, TILE)
    return (codes_next, tile_grads, threshold_grads)
```

```python
import functools

import jax
import jax.numpy as jnp
from jax import lax
from jax.experimental import pallas as pl
from jax.experimental.pallas import tpu as pltpu
from jax.sharding import PartitionSpec as P

MESH = pl.DeviceIdType.MESH
F32 = jnp.float32
BF16 = jnp.bfloat16
T = 128
V = 8


def swap(x):
    turned = pltpu.roll(x, V // 2, 1)
    rows = lax.broadcasted_iota(jnp.int32, x.shape, 1)
    return jnp.where(rows < V // 2, -turned, turned)


def nt(a, b):
    return lax.dot_general(a, b, (((1,), (1,)), ((), ())), preferred_element_type=F32)


def nn(a, b):
    return lax.dot_general(a, b, (((1,), (0,)), ((), ())), preferred_element_type=F32)


def tn(a, b):
    return lax.dot_general(a, b, (((0,), (0,)), ((), ())), preferred_element_type=F32)


def wait_bytes(ref, sem):
    pltpu.make_async_copy(ref, ref, sem).wait()


def kernel(
    n_dof, n_atom, slots, row_tiles, atom_tiles, groups,
    received, codes, tiles, coords, counts, group_ids, thresholds, cotangent,
    next_out, grads_out, thr_out,
    places, held, shares, rec,
    codes_send, codes_recv, corr_send, corr_recv, grad_send, grad_recv,
    codes_pick, grad_pick,
    part, pair, half, gather, resid, resid_share,
    sized, part_b, pair_b, half_b, gather_b, back, back_share,
    thr_part, thr_dof, thr_sum, thr_pair, thr_both, thr_atom,
    send, recv,
):
    p = lax.axis_index("dof")
    q = lax.axis_index("atom")
    chips = n_atom // 2
    chip, core = q // 2, q % 2
    rows = V * n_dof
    total = row_tiles * rows
    chunk = total // n_atom

    def dof_peer(j):
        return lax.rem(p + j, n_dof)

    def chip_peer(j):
        return lax.rem(chip + j, chips)

    mate = (p, chip * 2 + 1 - core)

    barrier = pltpu.get_barrier_semaphore()

    @pl.loop(1, n_dof)
    def _(j):
        pl.semaphore_signal(barrier, inc=1, device_id=(dof_peer(j), q), device_id_type=MESH)

    @pl.loop(1, chips)
    def _(j):
        pl.semaphore_signal(
            barrier, inc=1, device_id=(p, chip_peer(j) * 2 + core), device_id_type=MESH
        )

    pl.semaphore_signal(barrier, inc=1, device_id=mate, device_id_type=MESH)

    for k in range(atom_tiles):
        cols = slice(k * T, (k + 1) * T)
        held[k] = jnp.concatenate(
            [codes[0, :, cols].astype(F32), codes[1, :, cols].astype(F32)], axis=0
        )
    rec[...] = received[...].astype(F32)

    pl.semaphore_wait(barrier, n_dof - 1 + chips - 1 + 1)

    def remote(src, dst, s, device):
        return pltpu.make_async_remote_copy(
            src_ref=src, dst_ref=dst, send_sem=send.at[s], recv_sem=recv.at[s],
            device_id=device, device_id_type=MESH,
        )

    @pl.loop(1, n_dof)
    def _(j):
        remote(coords, places.at[p], 0, (dof_peer(j), q)).start()

    for l in range(slots):
        places[p, l, 0] = coords[l, 0]
        places[p, l, 1] = coords[l, 1]
    wait_bytes(places.at[pl.ds(0, n_dof - 1)], recv.at[0])

    def hot(flag):
        return jnp.where(flag, 1.0, 0.0).astype(F32)

    live = [hot(l < counts[0, 0]) for l in range(slots)]

    def pick_and_send(table, out, into, s):
        def build(peer):
            return jnp.concatenate(
                [table[places[peer, l, 1]] for l in range(slots)], axis=0
            ).astype(BF16)

        @pl.loop(1, n_dof)
        def _(j):
            peer = dof_peer(j)
            out[peer] = build(peer)
            remote(out.at[peer], into.at[p], s, (peer, q)).start()

        into[p] = build(p)
        wait_bytes(into.at[pl.ds(0, n_dof - 1)], recv.at[s])

    def apply(arrived, picked, dst):
        x = arrived[...].astype(F32)
        products = []
        for l in range(slots):
            xl = x[:, l * V : (l + 1) * V, :]
            plain = xl.reshape(rows, T).astype(BF16)
            turned = swap(xl).reshape(rows, T).astype(BF16)
            picked[l, :, :T] = plain
            picked[l, :, T:] = turned
            products.append(nt(plain, tiles[l, 0]) + nt(turned, tiles[l, 1]))
        for r in range(row_tiles):
            acc = products[0] * (live[0] * hot(coords[0, 0] == r))
            for l in range(1, slots):
                acc += products[l] * (live[l] * hot(coords[l, 0] == r))
            dst[r * rows : (r + 1) * rows, :] = acc.astype(dst.dtype)

    def sum_and_share(dst, pairing, halved, gathered, share, full, finish, s):
        n_half = total // 2
        mine = pl.ds(pl.multiple_of(core * n_half, n_half), n_half)
        theirs = pl.ds(pl.multiple_of((1 - core) * n_half, n_half), n_half)
        remote(dst.at[theirs], pairing, s, mate).start()
        wait_bytes(pairing, recv.at[s])
        halved[...] = (dst[mine, :].astype(F32) + pairing[...].astype(F32)).astype(halved.dtype)

        def rows_of(c):
            return pl.ds(pl.multiple_of(c * chunk, chunk), chunk)

        @pl.loop(1, chips)
        def _(j):
            c = chip_peer(j)
            remote(
                halved.at[rows_of(c)], gathered.at[chip], s + 1, (p, c * 2 + core)
            ).start()

        gathered[chip] = halved[rows_of(chip), :]
        wait_bytes(gathered.at[pl.ds(0, chips - 1)], recv.at[s + 1])
        acc = gathered[0].astype(F32)
        for c in range(1, chips):
            acc += gathered[c].astype(F32)
        share[...] = finish(acc).astype(BF16)
        first = core * n_half + chip * chunk
        full_rows = full.at[
            first // rows, pl.ds(pl.multiple_of(first % rows, chunk), chunk)
        ]
        n_tiles = row_tiles // 2
        full_half = full.at[pl.ds(core * n_tiles, n_tiles)]

        @pl.loop(1, chips)
        def _(j):
            remote(share, full_rows, s + 2, (p, chip_peer(j) * 2 + core)).start()

        full_rows[...] = share[...]
        wait_bytes(sized.at[pl.ds(0, (chips - 1) * chunk)], recv.at[s + 2])
        remote(full_half, full_half, s + 3, mate).start()
        wait_bytes(sized, recv.at[s + 3])

        wait_bytes(dst.at[pl.ds(0, n_half)], send.at[s])
        wait_bytes(gathered.at[pl.ds(0, chips - 1)], send.at[s + 1])
        wait_bytes(sized.at[pl.ds(0, (chips - 1) * chunk)], send.at[s + 2])
        wait_bytes(sized, send.at[s + 3])

    pick_and_send(held, codes_send, codes_recv, 1)
    apply(codes_recv, codes_pick, part)

    def minus_received(acc):
        first = (core * chips + chip) * chunk
        tile, inside = first // rows, first % rows
        snaps = pl.ds(pl.multiple_of(inside // 2, V), chunk // 2)
        cols = pl.ds(pl.multiple_of(tile * T, T), T)
        re, im = rec[0, snaps, cols], rec[1, snaps, cols]
        low = lax.broadcasted_iota(jnp.int32, (V, T), 0) < V // 2
        blocks = []
        for b in range(chunk // (2 * V)):
            a, c = re[b * V : (b + 1) * V], im[b * V : (b + 1) * V]
            blocks.append(jnp.where(low, a, pltpu.roll(c, V // 2, 0)))
            blocks.append(jnp.where(low, pltpu.roll(a, V // 2, 0), c))
        return jnp.concatenate(blocks, axis=0) - acc

    sum_and_share(part, pair, half, gather, resid_share, resid, minus_received, 2)

    def row_block(ref, l):
        return ref[coords[l, 0]]

    corr = []
    for l in range(slots):
        plain = row_block(resid, l)
        turned = (
            swap(plain.astype(F32).reshape(n_dof, V, T)).reshape(rows, T).astype(BF16)
        )
        g = (nn(plain, tiles[l, 0]) - nn(turned, tiles[l, 1])) * live[l]
        corr.append(g.reshape(n_dof, V, T))
    corr_send[...] = jnp.concatenate(corr, axis=1).astype(corr_send.dtype)

    @pl.loop(1, n_dof)
    def _(j):
        peer = dof_peer(j)
        remote(corr_send.at[peer], corr_recv.at[p], 6, (peer, q)).start()

    corr_recv[p] = corr_send[p]
    wait_bytes(corr_recv.at[pl.ds(0, n_dof - 1)], recv.at[6])

    def add_tile(j, acc):
        peer, l = j // slots, j % slots
        at = jnp.full((V, T), places[peer, l, 1], jnp.int32)
        v = corr_recv[peer, pl.ds(pl.multiple_of(l * V, V), V), :].astype(F32)
        return tuple(
            a + jnp.where(at == k, v, 0.0) for k, a in enumerate(acc)
        )

    zero = jnp.zeros((V, T), F32)
    sums = lax.fori_loop(0, n_dof * slots, add_tile, (zero,) * atom_tiles)

    thr = [zero] * groups
    for k in range(atom_tiles):
        cols = slice(k * T, (k + 1) * T)
        field = held[k] + sums[k]
        theta = jnp.full((V, T), thresholds[group_ids[k]], F32)
        cot = jnp.concatenate(
            [cotangent[0, :, cols].astype(F32), cotangent[1, :, cols].astype(F32)], axis=0
        )
        square = field * field
        magnitude = jnp.sqrt(square + pltpu.roll(square, V // 2, 0) + 1e-06)
        most = jnp.maximum(magnitude, theta)
        factor = jnp.maximum(magnitude - theta, 0.0) / most
        shrunk = (field * factor).astype(BF16)
        next_out[0, :, cols] = shrunk[: V // 2]
        next_out[1, :, cols] = shrunk[V // 2 :]
        product = cot * field
        pulled = (product + pltpu.roll(product, V // 2, 0)) / most
        above = jnp.where(magnitude > theta, 1.0, jnp.where(magnitude == theta, 0.5, 0.0))
        pulled = pulled * above
        grad = cot * factor + field * (pulled * (1.0 - factor) / magnitude)
        shares[k] = grad.astype(BF16).astype(F32)
        own = jnp.full((V, T), group_ids[k], jnp.int32)
        thr = [t - jnp.where(own == g, pulled, 0.0) for g, t in enumerate(thr)]

    pick_and_send(shares, grad_send, grad_recv, 7)

    for g in range(groups):
        thr_part[g : g + 1, :] = 0.5 * jnp.sum(thr[g], axis=0, keepdims=True)

    @pl.loop(1, n_dof)
    def _(j):
        remote(thr_part, thr_dof.at[p], 12, (dof_peer(j), q)).start()

    thr_dof[p] = thr_part[...]

    apply(grad_recv, grad_pick, part_b)
    wait_bytes(thr_dof.at[pl.ds(0, n_dof - 1)], recv.at[12])
    acc = thr_dof[0]
    for i in range(1, n_dof):
        acc += thr_dof[i]
    thr_sum[...] = acc
    remote(thr_sum, thr_pair, 13, mate).start()

    sum_and_share(part_b, pair_b, half_b, gather_b, back_share, back, lambda acc: acc, 8)

    wait_bytes(thr_pair, recv.at[13])
    thr_both[...] = thr_sum[...] + thr_pair[...]

    @pl.loop(1, chips)
    def _(j):
        remote(thr_both, thr_atom.at[chip], 14, (p, chip_peer(j) * 2 + core)).start()

    thr_atom[chip] = thr_both[...]

    for l in range(slots):
        left = tn(row_block(resid, l), grad_pick[l])
        right = tn(row_block(back, l), codes_pick[l])
        g = ((left - right) * live[l]).astype(BF16)
        grads_out[l, 0] = g[:, :T]
        grads_out[l, 1] = g[:, T:]

    wait_bytes(thr_atom.at[pl.ds(0, chips - 1)], recv.at[14])
    acc = thr_atom[0]
    for c in range(1, chips):
        acc += thr_atom[c]
    thr_out[...] = jnp.sum(acc, axis=1, keepdims=True)

    wait_bytes(places.at[pl.ds(0, n_dof - 1)], send.at[0])
    wait_bytes(codes_recv.at[pl.ds(0, n_dof - 1)], send.at[1])
    wait_bytes(corr_recv.at[pl.ds(0, n_dof - 1)], send.at[6])
    wait_bytes(grad_recv.at[pl.ds(0, n_dof - 1)], send.at[7])
    wait_bytes(thr_dof.at[pl.ds(0, n_dof - 1)], send.at[12])
    wait_bytes(thr_pair, send.at[13])
    wait_bytes(thr_atom.at[pl.ds(0, chips - 1)], send.at[14])


def local(n_dof, n_atom, received, codes, tiles, coords, counts, group_ids, thresholds, cotangent):
    slots = tiles.shape[2]
    row_tiles = received.shape[2] // T
    atom_tiles = codes.shape[2] // T
    groups = thresholds.shape[0]
    rows = V * n_dof
    total = row_tiles * rows
    chunk = total // n_atom
    chips = n_atom // 2
    vmem = pl.BlockSpec(memory_space=pltpu.VMEM)
    smem = pl.BlockSpec(memory_space=pltpu.SMEM)

    def exchange(dtype):
        return [pltpu.VMEM((n_dof, slots * V, T), dtype)] * 2

    def summing(dtype):
        return [
            pltpu.VMEM((total, T), dtype),
            pltpu.VMEM((total // 2, T), dtype),
            pltpu.VMEM((total // 2, T), dtype),
            pltpu.VMEM((chips, chunk, T), dtype),
            pltpu.VMEM((row_tiles, rows, T), BF16),
            pltpu.VMEM((chunk, T), BF16),
        ]

    out = pl.pallas_call(
        functools.partial(kernel, n_dof, n_atom, slots, row_tiles, atom_tiles, groups),
        out_shape=(
            jax.ShapeDtypeStruct(codes.shape, BF16),
            jax.ShapeDtypeStruct(tiles.shape[2:], BF16),
            jax.ShapeDtypeStruct((groups, 1), F32),
        ),
        in_specs=[vmem, vmem, vmem, smem, smem, smem, smem, vmem],
        out_specs=(vmem, vmem, vmem),
        scratch_shapes=[
            pltpu.SMEM((n_dof, slots, 2), jnp.int32),
            pltpu.VMEM((atom_tiles, V, T), F32),
            pltpu.VMEM((atom_tiles, V, T), F32),
            pltpu.VMEM(received.shape, F32),
            *exchange(BF16),
            *exchange(F32),
            *exchange(BF16),
            pltpu.VMEM((slots, rows, 2 * T), BF16),
            pltpu.VMEM((slots, rows, 2 * T), BF16),
            *summing(F32),
            pltpu.VMEM((total // 2, T), BF16),
            *summing(BF16),
            pltpu.VMEM((groups, T), F32),
            pltpu.VMEM((n_dof, groups, T), F32),
            pltpu.VMEM((groups, T), F32),
            pltpu.VMEM((groups, T), F32),
            pltpu.VMEM((groups, T), F32),
            pltpu.VMEM((chips, groups, T), F32),
            pltpu.SemaphoreType.DMA((15,)),
            pltpu.SemaphoreType.DMA((15,)),
        ],
        compiler_params=pltpu.CompilerParams(
            collective_id=0, has_side_effects=True, vmem_limit_bytes=32 * 1024 * 1024
        ),
    )(received, codes, tiles[0, 0], coords[0, 0], counts, group_ids, thresholds, cotangent)
    codes_next, tile_grads, threshold_grads = out
    return codes_next, tile_grads[None, None], threshold_grads[:, 0]


def solution(mesh):
    placed = (
        P(None, None, "dof"),
        P(None, "dof", "atom"),
        P("dof", "atom", None, None, None, None),
        P("dof", "atom", None, None),
        P("dof", "atom"),
        P("atom"),
        P(),
        P(None, "dof", "atom"),
    )
    return jax.shard_map(
        functools.partial(local, mesh.shape["dof"], mesh.shape["atom"]),
        mesh=mesh,
        in_specs=placed,
        out_specs=(P(None, "dof", "atom"), P("dof", "atom", None, None, None, None), P()),
        check_vma=False,
    )
```

```python
import functools

import jax
import jax.numpy as jnp
from jax import lax
from jax.experimental import pallas as pl
from jax.experimental.pallas import tpu as pltpu
from jax.sharding import PartitionSpec as P

MESH = pl.DeviceIdType.MESH
F32 = jnp.float32
BF16 = jnp.bfloat16
T = 128
V = 8


def swap(x):
    turned = pltpu.roll(x, V // 2, 1)
    rows = lax.broadcasted_iota(jnp.int32, x.shape, 1)
    return jnp.where(rows < V // 2, -turned, turned)


def nt(a, b):
    return lax.dot_general(a, b, (((1,), (1,)), ((), ())), preferred_element_type=F32)


def nn(a, b):
    return lax.dot_general(a, b, (((1,), (0,)), ((), ())), preferred_element_type=F32)


def tn(a, b):
    return lax.dot_general(a, b, (((0,), (0,)), ((), ())), preferred_element_type=F32)


def wait_bytes(ref, sem):
    pltpu.make_async_copy(ref, ref, sem).wait()


def entry(values, t):
    out = values[-1]
    for i in reversed(range(len(values) - 1)):
        out = jnp.where(t == i, values[i], out)
    return out


def kernel(
    n_dof, n_atom, slots, row_tiles, atom_tiles, groups,
    received_hbm, codes_hbm, tiles_hbm, coords_hbm, counts_hbm, ids_hbm, thresholds_hbm, cotangent_hbm,
    next_out, grads_out, thr_out,
    received, codes, tiles, cotangent, coords, counts, group_ids, thresholds,
    near, places, held, shares, rec,
    dense, dense_recv, blocks, codes_send, codes_recv,
    corr_send, corr_recv, grad_send, grad_recv, codes_pick, grad_pick,
    part, pair, half, gather, resid, resid_share,
    part_b, gather_b, back, back_share, lefts, sized,
    thr_part, thr_dof, thr_sum, thr_atom,
    send, recv, fetch,
):
    p = lax.axis_index("dof")
    q = lax.axis_index("atom")
    z_hi, z_lo = 4, 4
    ny, nx = n_dof // z_hi, n_atom // (2 * z_lo)
    chips = n_atom // 2
    chip, core = q // 2, q % 2
    y, zh = p // z_hi, p % z_hi
    x, zl = chip // z_lo, chip % z_lo
    rows = V * n_dof
    total = row_tiles * rows
    chunk = total // n_atom
    n_half = total // 2
    away = (2, 1, 3, 0)

    def dof_peer(t):
        dz, dy = entry(away, t // ny), (entry(away, t % ny) if ny > 1 else 0)
        return lax.rem(y + dy, ny) * z_hi + lax.rem(zh + dz, z_hi)

    def chip_peer(t):
        outer = (nx - 1) * z_lo
        dx = jnp.where(t < outer, entry(away[:3], t // z_lo), 0)
        end = jnp.where(zl < z_lo // 2, z_lo - 1 - t % z_lo, t % z_lo)
        to = jnp.where(t < outer, end, lax.rem(zl + t - outer + 1, z_lo))
        return lax.rem(x + dx, nx) * z_lo + to

    mate = (p, chip * 2 + 1 - core)

    fetches = [
        pltpu.make_async_copy(a, b, fetch.at[i])
        for i, (a, b) in enumerate([
            (coords_hbm, coords), (codes_hbm, codes), (tiles_hbm, tiles), (counts_hbm, counts),
            (received_hbm, received), (cotangent_hbm, cotangent), (ids_hbm, group_ids),
            (thresholds_hbm, thresholds),
        ])
    ]
    for f in fetches:
        f.start()

    barrier = pltpu.get_barrier_semaphore()

    def greet(device):
        pl.semaphore_signal(barrier, inc=1, device_id=device, device_id_type=MESH)

    @pl.loop(0, n_dof - 1)
    def _(t):
        greet((dof_peer(t), q))

    @pl.loop(0, chips - 1)
    def _(t):
        c = chip_peer(t)
        greet((p, c * 2))
        greet((p, c * 2 + 1))

    greet(mate)

    fetches[0].wait()
    fetches[1].wait()
    for k in range(atom_tiles):
        cols = slice(k * T, (k + 1) * T)
        tile = jnp.concatenate(
            [codes[0, :, cols].astype(F32), codes[1, :, cols].astype(F32)], axis=0
        )
        held[k] = tile
        blocks[zh, k] = tile
    dense[...] = held[...].reshape(atom_tiles * V, T).astype(BF16)

    pl.semaphore_wait(barrier, n_dof - 1 + n_atom - 1)

    def remote(src, dst, s, device, r=None):
        return pltpu.make_async_remote_copy(
            src_ref=src, dst_ref=dst, send_sem=send.at[s], recv_sem=recv.at[s if r is None else r],
            device_id=device, device_id_type=MESH,
        )

    leaving = []

    for dz in away[:-1]:
        to = lax.rem(zh + dz, z_hi)
        remote(dense, dense_recv.at[zh], 15 + dz, (y * z_hi + to, q), 15 + z_hi - dz).start()
        leaving.append((dense, 15 + dz))
    for dy in range(1, ny):
        to = lax.rem(y + dy, ny)
        remote(coords, near.at[y], 0, (to * z_hi + zh, q)).start()

    @pl.loop(0, n_dof - 1)
    def _(t):
        remote(coords, places.at[p], 1, (dof_peer(t), q)).start()

    leaving.append((places.at[pl.ds(0, n_dof - 1)], 1))
    for l in range(slots):
        for d in range(2):
            near[y, d, l] = coords[d, l]
            places[p, d, l] = coords[d, l]
    if ny > 1:
        wait_bytes(near.at[pl.ds(0, ny - 1)], recv.at[0])
        leaving.append((near.at[pl.ds(0, ny - 1)], 0))

    def build(table, named):
        return jnp.concatenate([table(named(l)) for l in range(slots)], axis=0).astype(BF16)

    for dz in (0, 1, 3, 2):
        z = lax.rem(zh + dz, z_hi)
        if dz:
            wait_bytes(dense_recv.at[z], recv.at[15 + dz])
            blocks[z] = dense_recv[z].astype(F32).reshape(atom_tiles, V, T)
        for dy in range(1, ny):
            to = lax.rem(y + dy, ny)
            codes_send[to, z] = build(lambda k, z=z: blocks[z, k], lambda l, to=to: near[to, 1, l])
            remote(codes_send.at[to, z], codes_recv.at[y * z_hi + z], 2, (to * z_hi + zh, q)).start()
        codes_recv[y * z_hi + z] = build(lambda k, z=z: blocks[z, k], lambda l: coords[1, l])
    fetches[2].wait()
    fetches[3].wait()
    fetches[4].wait()
    rec[...] = received[...].astype(F32)
    if ny > 1:
        wait_bytes(codes_recv.at[pl.ds(0, (ny - 1) * z_hi)], recv.at[2])
        leaving.append((codes_recv.at[pl.ds(0, (ny - 1) * z_hi)], 2))

    def hot(flag):
        return jnp.where(flag, 1.0, 0.0).astype(F32)

    live = [hot(l < counts[0, 0]) for l in range(slots)]

    def apply(arrived, picked, dst):
        v = arrived[...].astype(F32)
        products = []
        for l in range(slots):
            xl = v[:, l * V : (l + 1) * V, :]
            plain = xl.reshape(rows, T).astype(BF16)
            turned = swap(xl).reshape(rows, T).astype(BF16)
            picked[l, :, :T] = plain
            picked[l, :, T:] = turned
            products.append(nt(plain, tiles[l, 0]) + nt(turned, tiles[l, 1]))
        for r in range(row_tiles):
            acc = products[0] * (live[0] * hot(coords[0, 0] == r))
            for l in range(1, slots):
                acc += products[l] * (live[l] * hot(coords[0, l] == r))
            dst[r * rows : (r + 1) * rows, :] = acc.astype(dst.dtype)

    def rows_of(c):
        return pl.ds(pl.multiple_of(c * chunk, chunk), chunk)

    def to_all(make):
        @pl.loop(0, chips - 1)
        def _(t):
            c = chip_peer(t)
            for k in range(2):
                make(c, k).start()

        make(chip, 1 - core).start()

    def share_all(share, full, s):
        first = core * n_half + chip * chunk
        place = full.at[first // rows, pl.ds(pl.multiple_of(first % rows, chunk), chunk)]
        to_all(lambda c, k: remote(share, place, s, (p, c * 2 + k)))
        place[...] = share[...]
        leaving.append((sized.at[pl.ds(0, total - chunk)], s))

    apply(codes_recv, codes_pick, part)
    mine = pl.ds(pl.multiple_of(core * n_half, n_half), n_half)
    theirs = pl.ds(pl.multiple_of((1 - core) * n_half, n_half), n_half)
    remote(part.at[theirs], pair, 3, mate).start()
    wait_bytes(pair, recv.at[3])
    leaving.append((pair, 3))
    half[...] = part[mine, :] + pair[...]

    @pl.loop(0, chips - 1)
    def _(t):
        c = chip_peer(t)
        remote(half.at[rows_of(c)], gather.at[chip], 4, (p, c * 2 + core)).start()

    gather[chip] = half[rows_of(chip), :]
    wait_bytes(gather.at[pl.ds(0, chips - 1)], recv.at[4])
    leaving.append((gather.at[pl.ds(0, chips - 1)], 4))
    acc = gather[0]
    for c in range(1, chips):
        acc += gather[c]

    first = (core * chips + chip) * chunk
    snaps = pl.ds(pl.multiple_of(first % rows // 2, V), chunk // 2)
    cols = pl.ds(pl.multiple_of(first // rows * T, T), T)
    re, im = rec[0, snaps, cols], rec[1, snaps, cols]
    low = lax.broadcasted_iota(jnp.int32, (V, T), 0) < V // 2
    ordered = []
    for b in range(chunk // (2 * V)):
        a, c = re[b * V : (b + 1) * V], im[b * V : (b + 1) * V]
        ordered.append(jnp.where(low, a, pltpu.roll(c, V // 2, 0)))
        ordered.append(jnp.where(low, pltpu.roll(a, V // 2, 0), c))
    resid_share[...] = (jnp.concatenate(ordered, axis=0) - acc).astype(BF16)
    share_all(resid_share, resid, 5)
    wait_bytes(sized.at[pl.ds(0, total - chunk)], recv.at[5])

    def row_block(ref, l):
        return ref[coords[0, l]]

    corr = []
    for l in range(slots):
        plain = row_block(resid, l)
        turned = swap(plain.astype(F32).reshape(n_dof, V, T)).reshape(rows, T).astype(BF16)
        g = (nn(plain, tiles[l, 0]) - nn(turned, tiles[l, 1])) * live[l]
        corr.append(g.reshape(n_dof, V, T))
    corr_send[...] = jnp.concatenate(corr, axis=1).astype(corr_send.dtype)

    @pl.loop(0, n_dof - 1)
    def _(t):
        peer = dof_peer(t)
        remote(corr_send.at[peer], corr_recv.at[p], 6, (peer, q)).start()

    leaving.append((corr_recv.at[pl.ds(0, n_dof - 1)], 6))
    corr_recv[p] = corr_send[p]
    fetches[5].wait()
    fetches[6].wait()
    fetches[7].wait()
    wait_bytes(places.at[pl.ds(0, n_dof - 1)], recv.at[1])
    wait_bytes(corr_recv.at[pl.ds(0, n_dof - 1)], recv.at[6])

    def add_tile(j, acc):
        peer, l = j // slots, j % slots
        at = jnp.full((V, T), places[peer, 1, l], jnp.int32)
        v = corr_recv[peer, pl.ds(pl.multiple_of(l * V, V), V), :].astype(F32)
        return tuple(a + jnp.where(at == k, v, 0.0) for k, a in enumerate(acc))

    zero = jnp.zeros((V, T), F32)
    sums = lax.fori_loop(0, n_dof * slots, add_tile, (zero,) * atom_tiles)

    thr = [zero] * groups
    for k in range(atom_tiles):
        cols = slice(k * T, (k + 1) * T)
        field = held[k] + sums[k]
        theta = jnp.full((V, T), thresholds[group_ids[k]], F32)
        cot = jnp.concatenate(
            [cotangent[0, :, cols].astype(F32), cotangent[1, :, cols].astype(F32)], axis=0
        )
        square = field * field
        magnitude = jnp.sqrt(square + pltpu.roll(square, V // 2, 0) + 1e-06)
        most = jnp.maximum(magnitude, theta)
        factor = jnp.maximum(magnitude - theta, 0.0) / most
        shrunk = (field * factor).astype(BF16)
        next_out[0, :, cols] = shrunk[: V // 2]
        next_out[1, :, cols] = shrunk[V // 2 :]
        product = cot * field
        pulled = (product + pltpu.roll(product, V // 2, 0)) / most
        above = jnp.where(magnitude > theta, 1.0, jnp.where(magnitude == theta, 0.5, 0.0))
        pulled = pulled * above
        grad = cot * factor + field * (pulled * (1.0 - factor) / magnitude)
        shares[k] = grad.astype(BF16).astype(F32)
        own = jnp.full((V, T), group_ids[k], jnp.int32)
        thr = [t - jnp.where(own == g, pulled, 0.0) for g, t in enumerate(thr)]

    @pl.loop(0, n_dof - 1)
    def _(t):
        peer = dof_peer(t)
        grad_send[peer] = build(lambda k: shares[k], lambda l: places[peer, 1, l])
        remote(grad_send.at[peer], grad_recv.at[p], 7, (peer, q)).start()

    leaving.append((grad_recv.at[pl.ds(0, n_dof - 1)], 7))
    grad_recv[p] = build(lambda k: shares[k], lambda l: coords[1, l])

    lanes = lax.broadcasted_iota(jnp.int32, (1, T), 1)
    row = jnp.zeros((1, T), F32)
    for g in range(groups):
        row = jnp.where(lanes == g, 0.5 * jnp.sum(thr[g]), row)
    thr_part[...] = row

    @pl.loop(0, n_dof - 1)
    def _(t):
        remote(thr_part, thr_dof.at[p], 8, (dof_peer(t), q)).start()

    leaving.append((thr_dof.at[pl.ds(0, n_dof - 1)], 8))
    thr_dof[p] = thr_part[...]
    wait_bytes(grad_recv.at[pl.ds(0, n_dof - 1)], recv.at[7])

    apply(grad_recv, grad_pick, part_b)
    to_all(
        lambda c, k: remote(
            part_b.at[rows_of(k * chips + c)], gather_b.at[q], 9, (p, c * 2 + k)
        )
    )
    leaving.append((gather_b.at[pl.ds(0, n_atom - 1)], 9))
    gather_b[q] = part_b[rows_of(core * chips + chip), :]
    for l in range(slots):
        lefts[l] = tn(row_block(resid, l), grad_pick[l])
    wait_bytes(gather_b.at[pl.ds(0, n_atom - 1)], recv.at[9])
    acc = gather_b[0].astype(F32)
    for c in range(1, n_atom):
        acc += gather_b[c].astype(F32)
    back_share[...] = acc.astype(BF16)
    share_all(back_share, back, 10)

    wait_bytes(thr_dof.at[pl.ds(0, n_dof - 1)], recv.at[8])
    row = thr_dof[0]
    for i in range(1, n_dof):
        row += thr_dof[i]
    thr_sum[...] = row
    to_all(lambda c, k: remote(thr_sum, thr_atom.at[q], 11, (p, c * 2 + k)))
    leaving.append((thr_atom.at[pl.ds(0, n_atom - 1)], 11))
    thr_atom[q] = row

    wait_bytes(sized.at[pl.ds(0, total - chunk)], recv.at[10])
    for l in range(slots):
        right = tn(row_block(back, l), codes_pick[l])
        g = ((lefts[l] - right) * live[l]).astype(BF16)
        grads_out[l, 0] = g[:, :T]
        grads_out[l, 1] = g[:, T:]

    wait_bytes(thr_atom.at[pl.ds(0, n_atom - 1)], recv.at[11])
    row = thr_atom[0]
    for c in range(1, n_atom):
        row += thr_atom[c]
    thr_out[...] = row

    for ref, s in leaving:
        wait_bytes(ref, send.at[s])


def local(n_dof, n_atom, received, codes, tiles, coords, counts, group_ids, thresholds, cotangent):
    slots = tiles.shape[2]
    row_tiles = received.shape[2] // T
    atom_tiles = codes.shape[2] // T
    groups = thresholds.shape[0]
    rows = V * n_dof
    total = row_tiles * rows
    chunk = total // n_atom
    chips = n_atom // 2
    z_hi = 4
    vmem = pl.BlockSpec(memory_space=pltpu.VMEM)
    hbm = pl.BlockSpec(memory_space=pltpu.HBM)

    out = pl.pallas_call(
        functools.partial(kernel, n_dof, n_atom, slots, row_tiles, atom_tiles, groups),
        out_shape=(
            jax.ShapeDtypeStruct(codes.shape, BF16),
            jax.ShapeDtypeStruct(tiles.shape[2:], BF16),
            jax.ShapeDtypeStruct((1, T), F32),
        ),
        in_specs=[hbm] * 8,
        out_specs=(vmem, vmem, vmem),
        scratch_shapes=[
            pltpu.VMEM(received.shape, BF16),
            pltpu.VMEM(codes.shape, BF16),
            pltpu.VMEM(tiles.shape[2:], BF16),
            pltpu.VMEM(codes.shape, BF16),
            pltpu.SMEM((2, slots), jnp.int32),
            pltpu.SMEM(counts.shape, jnp.int32),
            pltpu.SMEM(group_ids.shape, jnp.int32),
            pltpu.SMEM(thresholds.shape, F32),
            pltpu.SMEM((n_dof // z_hi, 2, slots), jnp.int32),
            pltpu.SMEM((n_dof, 2, slots), jnp.int32),
            pltpu.VMEM((atom_tiles, V, T), F32),
            pltpu.VMEM((atom_tiles, V, T), F32),
            pltpu.VMEM(received.shape, F32),
            pltpu.VMEM((atom_tiles * V, T), BF16),
            pltpu.VMEM((z_hi, atom_tiles * V, T), BF16),
            pltpu.VMEM((z_hi, atom_tiles, V, T), F32),
            pltpu.VMEM((n_dof // z_hi, z_hi, slots * V, T), BF16),
            pltpu.VMEM((n_dof, slots * V, T), BF16),
            pltpu.VMEM((n_dof, slots * V, T), F32),
            pltpu.VMEM((n_dof, slots * V, T), F32),
            pltpu.VMEM((n_dof, slots * V, T), BF16),
            pltpu.VMEM((n_dof, slots * V, T), BF16),
            pltpu.VMEM((slots, rows, 2 * T), BF16),
            pltpu.VMEM((slots, rows, 2 * T), BF16),
            pltpu.VMEM((total, T), F32),
            pltpu.VMEM((total // 2, T), F32),
            pltpu.VMEM((total // 2, T), F32),
            pltpu.VMEM((chips, chunk, T), F32),
            pltpu.VMEM((row_tiles, rows, T), BF16),
            pltpu.VMEM((chunk, T), BF16),
            pltpu.VMEM((total, T), BF16),
            pltpu.VMEM((n_atom, chunk, T), BF16),
            pltpu.VMEM((row_tiles, rows, T), BF16),
            pltpu.VMEM((chunk, T), BF16),
            pltpu.VMEM((slots, T, 2 * T), F32),
            pltpu.VMEM((total, T), BF16),
            pltpu.VMEM((1, T), F32),
            pltpu.VMEM((n_dof, 1, T), F32),
            pltpu.VMEM((1, T), F32),
            pltpu.VMEM((n_atom, 1, T), F32),
            pltpu.SemaphoreType.DMA((19,)),
            pltpu.SemaphoreType.DMA((19,)),
            pltpu.SemaphoreType.DMA((8,)),
        ],
        compiler_params=pltpu.CompilerParams(
            collective_id=0, has_side_effects=True, vmem_limit_bytes=62 * 1024 * 1024
        ),
    )(received, codes, tiles[0, 0], coords[0, 0].T, counts, group_ids, thresholds, cotangent)
    codes_next, tile_grads, threshold_grads = out
    return codes_next, tile_grads[None, None], threshold_grads[0, :groups]


def solution(mesh):
    placed = (
        P(None, None, "dof"),
        P(None, "dof", "atom"),
        P("dof", "atom", None, None, None, None),
        P("dof", "atom", None, None),
        P("dof", "atom"),
        P("atom"),
        P(),
        P(None, "dof", "atom"),
    )
    return jax.shard_map(
        functools.partial(local, mesh.shape["dof"], mesh.shape["atom"]),
        mesh=mesh,
        in_specs=placed,
        out_specs=(P(None, "dof", "atom"), P("dof", "atom", None, None, None, None), P()),
        check_vma=False,
    )
```

```python
import functools

import jax
import jax.numpy as jnp
from jax import lax
from jax.experimental import pallas as pl
from jax.experimental.pallas import tpu as pltpu
from jax.sharding import PartitionSpec as P

MESH = pl.DeviceIdType.MESH
F32 = jnp.float32
BF16 = jnp.bfloat16
STEPS = 32000.0
T = 128
V = 8


def swap(x):
    turned = pltpu.roll(x, V // 2, 1)
    rows = lax.broadcasted_iota(jnp.int32, x.shape, 1)
    return jnp.where(rows < V // 2, -turned, turned)


def nt(a, b):
    return lax.dot_general(a, b, (((1,), (1,)), ((), ())), preferred_element_type=F32)


def nn(a, b):
    return lax.dot_general(a, b, (((1,), (0,)), ((), ())), preferred_element_type=F32)


def tn(a, b):
    return lax.dot_general(a, b, (((0,), (0,)), ((), ())), preferred_element_type=F32)


def wait_bytes(ref, sem):
    pltpu.make_async_copy(ref, ref, sem).wait()


def entry(values, t):
    out = values[-1]
    for i in reversed(range(len(values) - 1)):
        out = jnp.where(t == i, values[i], out)
    return out


def kernel(
    n_dof, n_atom, slots, row_tiles, atom_tiles, groups,
    received_hbm, codes_hbm, tiles_hbm, coords_hbm, counts_hbm, ids_hbm, thresholds_hbm, cotangent_hbm,
    next_out, grads_out, thr_out,
    received, codes, tiles, cotangent, coords, counts, group_ids, thresholds,
    near, places, held, shares, rec, next_kept, grads_kept,
    dense, dense_recv, blocks, codes_send, codes_recv,
    corr_send, corr_recv, scale_send, scale_recv, grad_send, grad_recv, codes_pick, grad_pick,
    part, pair, half, gather, resid, resid_share,
    part_b, gather_b, back, back_share, lefts, sized,
    thr_part, thr_dof, thr_sum, thr_atom,
    send, recv, fetch, store,
):
    p = lax.axis_index("dof")
    q = lax.axis_index("atom")
    z_hi, z_lo = 4, 4
    ny, nx = n_dof // z_hi, n_atom // (2 * z_lo)
    chips = n_atom // 2
    chip, core = q // 2, q % 2
    y, zh = p // z_hi, p % z_hi
    x, zl = chip // z_lo, chip % z_lo
    rows = V * n_dof
    total = row_tiles * rows
    chunk = total // n_atom
    n_half = total // 2
    away = (2, 1, 3, 0)

    def dof_peer(t):
        dz, dy = entry(away, t // ny), (entry(away, t % ny) if ny > 1 else 0)
        return lax.rem(y + dy, ny) * z_hi + lax.rem(zh + dz, z_hi)

    def chip_peer(t):
        outer = (nx - 1) * z_lo
        dx = jnp.where(t < outer, entry(away[:3], t // z_lo), 0)
        end = jnp.where(zl < z_lo // 2, z_lo - 1 - t % z_lo, t % z_lo)
        to = jnp.where(t < outer, end, lax.rem(zl + t - outer + 1, z_lo))
        return lax.rem(x + dx, nx) * z_lo + to

    mate = (p, chip * 2 + 1 - core)

    fetches = [
        pltpu.make_async_copy(a, b, fetch.at[i])
        for i, (a, b) in enumerate([
            (coords_hbm, coords), (codes_hbm, codes), (tiles_hbm, tiles), (counts_hbm, counts),
            (received_hbm, received), (cotangent_hbm, cotangent), (ids_hbm, group_ids),
            (thresholds_hbm, thresholds),
        ])
    ]
    for f in fetches:
        f.start()

    barrier = pltpu.get_barrier_semaphore()

    def greet(device):
        pl.semaphore_signal(barrier, inc=1, device_id=device, device_id_type=MESH)

    @pl.loop(0, n_dof - 1)
    def _(t):
        greet((dof_peer(t), q))

    @pl.loop(0, chips - 1)
    def _(t):
        c = chip_peer(t)
        greet((p, c * 2))
        greet((p, c * 2 + 1))

    greet(mate)

    fetches[0].wait()
    fetches[1].wait()
    for k in range(atom_tiles):
        cols = slice(k * T, (k + 1) * T)
        tile = jnp.concatenate(
            [codes[0, :, cols].astype(F32), codes[1, :, cols].astype(F32)], axis=0
        )
        held[k] = tile
        blocks[zh, k] = tile
    dense[...] = held[...].reshape(atom_tiles * V, T).astype(BF16)

    pl.semaphore_wait(barrier, n_dof - 1 + n_atom - 1)

    def remote(src, dst, s, device, r=None):
        return pltpu.make_async_remote_copy(
            src_ref=src, dst_ref=dst, send_sem=send.at[s], recv_sem=recv.at[s if r is None else r],
            device_id=device, device_id_type=MESH,
        )

    leaving = []

    for dz in away[:-1]:
        to = lax.rem(zh + dz, z_hi)
        remote(dense, dense_recv.at[zh], 15 + dz, (y * z_hi + to, q), 15 + z_hi - dz).start()
        leaving.append((dense, 15 + dz))
    for dy in range(1, ny):
        to = lax.rem(y + dy, ny)
        remote(coords, near.at[y], 0, (to * z_hi + zh, q)).start()

    @pl.loop(0, n_dof - 1)
    def _(t):
        remote(coords, places.at[p], 1, (dof_peer(t), q)).start()

    leaving.append((places.at[pl.ds(0, n_dof - 1)], 1))
    for l in range(slots):
        for d in range(2):
            near[y, d, l] = coords[d, l]
            places[p, d, l] = coords[d, l]
    if ny > 1:
        wait_bytes(near.at[pl.ds(0, ny - 1)], recv.at[0])
        leaving.append((near.at[pl.ds(0, ny - 1)], 0))

    def build(table, named):
        return jnp.concatenate([table(named(l)) for l in range(slots)], axis=0).astype(BF16)

    for dz in (0, 1, 3, 2):
        z = lax.rem(zh + dz, z_hi)
        if dz:
            wait_bytes(dense_recv.at[z], recv.at[15 + dz])
            blocks[z] = dense_recv[z].astype(F32).reshape(atom_tiles, V, T)
        for dy in range(1, ny):
            to = lax.rem(y + dy, ny)
            codes_send[to, z] = build(lambda k, z=z: blocks[z, k], lambda l, to=to: near[to, 1, l])
            remote(codes_send.at[to, z], codes_recv.at[y * z_hi + z], 2, (to * z_hi + zh, q)).start()
        codes_recv[y * z_hi + z] = build(lambda k, z=z: blocks[z, k], lambda l: coords[1, l])
    fetches[2].wait()
    fetches[3].wait()
    fetches[4].wait()
    rec[...] = received[...].astype(F32)
    if ny > 1:
        wait_bytes(codes_recv.at[pl.ds(0, (ny - 1) * z_hi)], recv.at[2])
        leaving.append((codes_recv.at[pl.ds(0, (ny - 1) * z_hi)], 2))

    def hot(flag):
        return jnp.where(flag, 1.0, 0.0).astype(F32)

    live = [hot(l < counts[0, 0]) for l in range(slots)]

    def apply(arrived, picked, dst):
        v = arrived[...].astype(F32)
        products = []
        for l in range(slots):
            xl = v[:, l * V : (l + 1) * V, :]
            plain = xl.reshape(rows, T).astype(BF16)
            turned = swap(xl).reshape(rows, T).astype(BF16)
            picked[l, :, :T] = plain
            picked[l, :, T:] = turned
            products.append(nt(plain, tiles[l, 0]) + nt(turned, tiles[l, 1]))
        for r in range(row_tiles):
            acc = products[0] * (live[0] * hot(coords[0, 0] == r))
            for l in range(1, slots):
                acc += products[l] * (live[l] * hot(coords[0, l] == r))
            dst[r * rows : (r + 1) * rows, :] = acc.astype(dst.dtype)

    def rows_of(c):
        return pl.ds(pl.multiple_of(c * chunk, chunk), chunk)

    def to_all(make):
        @pl.loop(0, chips - 1)
        def _(t):
            c = chip_peer(t)
            for k in range(2):
                make(c, k).start()

        make(chip, 1 - core).start()

    def share_all(share, full, s):
        first = core * n_half + chip * chunk
        place = full.at[first // rows, pl.ds(pl.multiple_of(first % rows, chunk), chunk)]
        to_all(lambda c, k: remote(share, place, s, (p, c * 2 + k)))
        place[...] = share[...]
        leaving.append((sized.at[pl.ds(0, total - chunk)], s))

    apply(codes_recv, codes_pick, part)
    mine = pl.ds(pl.multiple_of(core * n_half, n_half), n_half)
    theirs = pl.ds(pl.multiple_of((1 - core) * n_half, n_half), n_half)
    remote(part.at[theirs], pair, 3, mate).start()
    wait_bytes(pair, recv.at[3])
    leaving.append((pair, 3))
    half[...] = part[mine, :] + pair[...]

    @pl.loop(0, chips - 1)
    def _(t):
        c = chip_peer(t)
        remote(half.at[rows_of(c)], gather.at[chip], 4, (p, c * 2 + core)).start()

    gather[chip] = half[rows_of(chip), :]
    wait_bytes(gather.at[pl.ds(0, chips - 1)], recv.at[4])
    leaving.append((gather.at[pl.ds(0, chips - 1)], 4))
    acc = gather[0]
    for c in range(1, chips):
        acc += gather[c]

    first = (core * chips + chip) * chunk
    snaps = pl.ds(pl.multiple_of(first % rows // 2, V), chunk // 2)
    cols = pl.ds(pl.multiple_of(first // rows * T, T), T)
    re, im = rec[0, snaps, cols], rec[1, snaps, cols]
    low = lax.broadcasted_iota(jnp.int32, (V, T), 0) < V // 2
    ordered = []
    for b in range(chunk // (2 * V)):
        a, c = re[b * V : (b + 1) * V], im[b * V : (b + 1) * V]
        ordered.append(jnp.where(low, a, pltpu.roll(c, V // 2, 0)))
        ordered.append(jnp.where(low, pltpu.roll(a, V // 2, 0), c))
    resid_share[...] = (jnp.concatenate(ordered, axis=0) - acc).astype(BF16)
    share_all(resid_share, resid, 5)
    wait_bytes(sized.at[pl.ds(0, total - chunk)], recv.at[5])

    def row_block(ref, l):
        return ref[coords[0, l]]

    corr = []
    for l in range(slots):
        plain = row_block(resid, l)
        turned = swap(plain.astype(F32).reshape(n_dof, V, T)).reshape(rows, T).astype(BF16)
        g = (nn(plain, tiles[l, 0]) - nn(turned, tiles[l, 1])) * live[l]
        corr.append(g.reshape(n_dof, V, T))
    corr = jnp.concatenate(corr, axis=1)
    most = jnp.maximum(jnp.max(jnp.abs(corr), axis=1, keepdims=True), 1e-30)
    corr_send[...] = jnp.round(corr * (STEPS / most)).astype(jnp.int32).astype(jnp.int16)
    scale_send[...] = most * (1.0 / STEPS)

    @pl.loop(0, n_dof - 1)
    def _(t):
        peer = dof_peer(t)
        remote(corr_send.at[peer], corr_recv.at[p], 6, (peer, q)).start()
        remote(scale_send.at[peer], scale_recv.at[p], 12, (peer, q)).start()

    leaving.append((corr_recv.at[pl.ds(0, n_dof - 1)], 6))
    leaving.append((scale_recv.at[pl.ds(0, n_dof - 1)], 12))
    corr_recv[p] = corr_send[p]
    scale_recv[p] = scale_send[p]
    fetches[5].wait()
    fetches[6].wait()
    fetches[7].wait()
    wait_bytes(places.at[pl.ds(0, n_dof - 1)], recv.at[1])
    wait_bytes(corr_recv.at[pl.ds(0, n_dof - 1)], recv.at[6])
    wait_bytes(scale_recv.at[pl.ds(0, n_dof - 1)], recv.at[12])

    def add_tiles(peer, acc):
        tiles_in = corr_recv[peer].astype(jnp.int32).astype(F32) * scale_recv[peer]
        for l in range(slots):
            at = jnp.full((V, T), places[peer, 1, l], jnp.int32)
            v = tiles_in[l * V : (l + 1) * V]
            acc = tuple(a + jnp.where(at == k, v, 0.0) for k, a in enumerate(acc))
        return acc

    zero = jnp.zeros((V, T), F32)
    sums = lax.fori_loop(0, n_dof, add_tiles, (zero,) * atom_tiles)

    thr = [zero] * groups
    for k in range(atom_tiles):
        cols = slice(k * T, (k + 1) * T)
        field = held[k] + sums[k]
        theta = jnp.full((V, T), thresholds[group_ids[k]], F32)
        cot = jnp.concatenate(
            [cotangent[0, :, cols].astype(F32), cotangent[1, :, cols].astype(F32)], axis=0
        )
        square = field * field
        magnitude = jnp.sqrt(square + pltpu.roll(square, V // 2, 0) + 1e-06)
        most = jnp.maximum(magnitude, theta)
        factor = jnp.maximum(magnitude - theta, 0.0) / most
        shrunk = (field * factor).astype(BF16)
        next_kept[0, :, cols] = shrunk[: V // 2]
        next_kept[1, :, cols] = shrunk[V // 2 :]
        product = cot * field
        pulled = (product + pltpu.roll(product, V // 2, 0)) / most
        above = jnp.where(magnitude > theta, 1.0, jnp.where(magnitude == theta, 0.5, 0.0))
        pulled = pulled * above
        grad = cot * factor + field * (pulled * (1.0 - factor) / magnitude)
        shares[k] = grad.astype(BF16).astype(F32)
        own = jnp.full((V, T), group_ids[k], jnp.int32)
        thr = [t - jnp.where(own == g, pulled, 0.0) for g, t in enumerate(thr)]

    stores = [pltpu.make_async_copy(next_kept, next_out, fetch.at[1])]
    stores[0].start()

    @pl.loop(0, n_dof - 1)
    def _(t):
        peer = dof_peer(t)
        grad_send[peer] = build(lambda k: shares[k], lambda l: places[peer, 1, l])
        remote(grad_send.at[peer], grad_recv.at[p], 7, (peer, q)).start()

    leaving.append((grad_recv.at[pl.ds(0, n_dof - 1)], 7))
    grad_recv[p] = build(lambda k: shares[k], lambda l: coords[1, l])

    lanes = lax.broadcasted_iota(jnp.int32, (1, T), 1)
    row = jnp.zeros((1, T), F32)
    for g in range(groups):
        row = jnp.where(lanes == g, 0.5 * jnp.sum(thr[g]), row)
    thr_part[...] = row

    @pl.loop(0, n_dof - 1)
    def _(t):
        remote(thr_part, thr_dof.at[p], 8, (dof_peer(t), q)).start()

    leaving.append((thr_dof.at[pl.ds(0, n_dof - 1)], 8))
    thr_dof[p] = thr_part[...]
    wait_bytes(grad_recv.at[pl.ds(0, n_dof - 1)], recv.at[7])

    apply(grad_recv, grad_pick, part_b)
    to_all(
        lambda c, k: remote(
            part_b.at[rows_of(k * chips + c)], gather_b.at[q], 9, (p, c * 2 + k)
        )
    )
    leaving.append((gather_b.at[pl.ds(0, n_atom - 1)], 9))
    gather_b[q] = part_b[rows_of(core * chips + chip), :]
    for l in range(slots):
        lefts[l] = tn(row_block(resid, l), grad_pick[l])
    wait_bytes(gather_b.at[pl.ds(0, n_atom - 1)], recv.at[9])
    acc = gather_b[0].astype(F32)
    for c in range(1, n_atom):
        acc += gather_b[c].astype(F32)
    back_share[...] = acc.astype(BF16)
    share_all(back_share, back, 10)

    wait_bytes(thr_dof.at[pl.ds(0, n_dof - 1)], recv.at[8])
    row = thr_dof[0]
    for i in range(1, n_dof):
        row += thr_dof[i]
    thr_sum[...] = row
    to_all(lambda c, k: remote(thr_sum, thr_atom.at[q], 11, (p, c * 2 + k)))
    leaving.append((thr_atom.at[pl.ds(0, n_atom - 1)], 11))
    thr_atom[q] = row

    wait_bytes(sized.at[pl.ds(0, total - chunk)], recv.at[10])
    for l in range(slots):
        right = tn(row_block(back, l), codes_pick[l])
        g = ((lefts[l] - right) * live[l]).astype(BF16)
        grads_kept[l, 0] = g[:, :T]
        grads_kept[l, 1] = g[:, T:]
        stores.append(pltpu.make_async_copy(grads_kept.at[l], grads_out.at[l], store.at[l]))
        stores[-1].start()

    wait_bytes(thr_atom.at[pl.ds(0, n_atom - 1)], recv.at[11])
    row = thr_atom[0]
    for c in range(1, n_atom):
        row += thr_atom[c]
    for g in range(groups):
        thr_out[g] = jnp.sum(jnp.where(lanes == g, row, 0.0))

    for copy in stores:
        copy.wait()
    for ref, s in leaving:
        wait_bytes(ref, send.at[s])


def hand_over(a, b, c, a_out, b_out, c_out, a_kept, b_kept, c_kept, sem):
    n = b.shape[0]
    parts = [(b.at[l], b_kept.at[l], b_out.at[l]) for l in range(n)]
    parts += [(a, a_kept, a_out), (c, c_kept, c_out)]
    loads = [pltpu.make_async_copy(x, k, sem.at[0, i]) for i, (x, k, _) in enumerate(parts)]
    stores = [pltpu.make_async_copy(k, y, sem.at[1, i]) for i, (_, k, y) in enumerate(parts)]
    for copy in loads:
        copy.start()
    for load, copy in zip(loads, stores):
        load.wait()
        copy.start()
    for copy in stores:
        copy.wait()


def local(n_dof, n_atom, received, codes, tiles, coords, counts, group_ids, thresholds, cotangent):
    slots = tiles.shape[2]
    row_tiles = received.shape[2] // T
    atom_tiles = codes.shape[2] // T
    groups = thresholds.shape[0]
    rows = V * n_dof
    total = row_tiles * rows
    chunk = total // n_atom
    chips = n_atom // 2
    z_hi = 4
    hbm = pl.BlockSpec(memory_space=pltpu.HBM)

    out = pl.pallas_call(
        functools.partial(kernel, n_dof, n_atom, slots, row_tiles, atom_tiles, groups),
        out_shape=(
            jax.ShapeDtypeStruct(codes.shape, BF16),
            jax.ShapeDtypeStruct(tiles.shape[2:], BF16),
            jax.ShapeDtypeStruct((groups,), F32),
        ),
        in_specs=[hbm] * 8,
        out_specs=(hbm, hbm, pl.BlockSpec(memory_space=pltpu.SMEM)),
        scratch_shapes=[
            pltpu.VMEM(received.shape, BF16),
            pltpu.VMEM(codes.shape, BF16),
            pltpu.VMEM(tiles.shape[2:], BF16),
            pltpu.VMEM(codes.shape, BF16),
            pltpu.SMEM((2, slots), jnp.int32),
            pltpu.SMEM(counts.shape, jnp.int32),
            pltpu.SMEM(group_ids.shape, jnp.int32),
            pltpu.SMEM(thresholds.shape, F32),
            pltpu.SMEM((n_dof // z_hi, 2, slots), jnp.int32),
            pltpu.SMEM((n_dof, 2, slots), jnp.int32),
            pltpu.VMEM((atom_tiles, V, T), F32),
            pltpu.VMEM((atom_tiles, V, T), F32),
            pltpu.VMEM(received.shape, F32),
            pltpu.VMEM(codes.shape, BF16),
            pltpu.VMEM(tiles.shape[2:], BF16),
            pltpu.VMEM((atom_tiles * V, T), BF16),
            pltpu.VMEM((z_hi, atom_tiles * V, T), BF16),
            pltpu.VMEM((z_hi, atom_tiles, V, T), F32),
            pltpu.VMEM((n_dof // z_hi, z_hi, slots * V, T), BF16),
            pltpu.VMEM((n_dof, slots * V, T), BF16),
            pltpu.VMEM((n_dof, slots * V, T), jnp.int16),
            pltpu.VMEM((n_dof, slots * V, T), jnp.int16),
            pltpu.VMEM((n_dof, 1, T), F32),
            pltpu.VMEM((n_dof, 1, T), F32),
            pltpu.VMEM((n_dof, slots * V, T), BF16),
            pltpu.VMEM((n_dof, slots * V, T), BF16),
            pltpu.VMEM((slots, rows, 2 * T), BF16),
            pltpu.VMEM((slots, rows, 2 * T), BF16),
            pltpu.VMEM((total, T), F32),
            pltpu.VMEM((total // 2, T), F32),
            pltpu.VMEM((total // 2, T), F32),
            pltpu.VMEM((chips, chunk, T), F32),
            pltpu.VMEM((row_tiles, rows, T), BF16),
            pltpu.VMEM((chunk, T), BF16),
            pltpu.VMEM((total, T), BF16),
            pltpu.VMEM((n_atom, chunk, T), BF16),
            pltpu.VMEM((row_tiles, rows, T), BF16),
            pltpu.VMEM((chunk, T), BF16),
            pltpu.VMEM((slots, T, 2 * T), F32),
            pltpu.VMEM((total, T), BF16),
            pltpu.VMEM((1, T), F32),
            pltpu.VMEM((n_dof, 1, T), F32),
            pltpu.VMEM((1, T), F32),
            pltpu.VMEM((n_atom, 1, T), F32),
            pltpu.SemaphoreType.DMA((19,)),
            pltpu.SemaphoreType.DMA((19,)),
            pltpu.SemaphoreType.DMA((8,)),
            pltpu.SemaphoreType.DMA((slots,)),
        ],
        compiler_params=pltpu.CompilerParams(
            collective_id=0, has_side_effects=True, vmem_limit_bytes=62 * 1024 * 1024
        ),
    )(received, codes, tiles[0, 0], coords[0, 0].T, counts, group_ids, thresholds, cotangent)
    codes_next, tile_grads, threshold_grads = pl.pallas_call(
        hand_over,
        out_shape=tuple(jax.ShapeDtypeStruct(o.shape, o.dtype) for o in out),
        in_specs=[hbm] * 3,
        out_specs=(hbm,) * 3,
        scratch_shapes=[
            pltpu.VMEM(codes.shape, BF16),
            pltpu.VMEM(tiles.shape[2:], BF16),
            pltpu.SMEM((groups,), F32),
            pltpu.SemaphoreType.DMA((2, slots + 2)),
        ],
        compiler_params=pltpu.CompilerParams(vmem_limit_bytes=62 * 1024 * 1024),
    )(*out)
    return codes_next, tile_grads[None, None], threshold_grads


def solution(mesh):
    placed = (
        P(None, None, "dof"),
        P(None, "dof", "atom"),
        P("dof", "atom", None, None, None, None),
        P("dof", "atom", None, None),
        P("dof", "atom"),
        P("atom"),
        P(),
        P(None, "dof", "atom"),
    )
    return jax.shard_map(
        functools.partial(local, mesh.shape["dof"], mesh.shape["atom"]),
        mesh=mesh,
        in_specs=placed,
        out_specs=(P(None, "dof", "atom"), P("dof", "atom", None, None, None, None), P()),
        check_vma=False,
    )
```

```python
import functools

import jax
import jax.numpy as jnp
from jax import lax
from jax.experimental import pallas as pl
from jax.experimental.pallas import tpu as pltpu
from jax.sharding import PartitionSpec as P

MESH = pl.DeviceIdType.MESH
F32 = jnp.float32
BF16 = jnp.bfloat16
STEPS = 32000.0
T = 128
V = 8


def swap(x):
    turned = pltpu.roll(x, V // 2, 1)
    rows = lax.broadcasted_iota(jnp.int32, x.shape, 1)
    return jnp.where(rows < V // 2, -turned, turned)


def nt(a, b):
    return lax.dot_general(a, b, (((1,), (1,)), ((), ())), preferred_element_type=F32)


def nn(a, b):
    return lax.dot_general(a, b, (((1,), (0,)), ((), ())), preferred_element_type=F32)


def tn(a, b):
    return lax.dot_general(a, b, (((0,), (0,)), ((), ())), preferred_element_type=F32)


def wait_bytes(ref, sem):
    pltpu.make_async_copy(ref, ref, sem).wait()


def entry(values, t):
    out = values[-1]
    for i in reversed(range(len(values) - 1)):
        out = jnp.where(t == i, values[i], out)
    return out


def kernel(
    n_dof, n_atom, slots, row_tiles, atom_tiles, groups,
    received_hbm, codes_hbm, tiles_hbm, coords_hbm, counts_hbm, ids_hbm, thresholds_hbm, cotangent_hbm,
    next_out, grads_out, thr_out,
    received, codes, tiles, cotangent, coords, counts, group_ids, thresholds,
    near, places, held, shares, rec, next_kept, grads_kept,
    dense, dense_recv, blocks, codes_send, codes_recv,
    corr_send, corr_recv, scale_send, scale_recv, grad_send, grad_recv, codes_pick, grad_pick,
    part, part_scale, gather, gather_scale, resid, resid_share,
    part_b, gather_b, back, back_share, lefts, sized,
    thr_part, thr_dof, thr_sum, thr_atom,
    send, recv, fetch, store,
):
    p = lax.axis_index("dof")
    q = lax.axis_index("atom")
    z_hi, z_lo = 4, 4
    ny, nx = n_dof // z_hi, n_atom // (2 * z_lo)
    chips = n_atom // 2
    chip, core = q // 2, q % 2
    y, zh = p // z_hi, p % z_hi
    x, zl = chip // z_lo, chip % z_lo
    rows = V * n_dof
    total = row_tiles * rows
    chunk = total // n_atom
    n_half = total // 2
    away = (2, 1, 3, 0)

    def dof_peer(t):
        dz, dy = entry(away, t // ny), (entry(away, t % ny) if ny > 1 else 0)
        return lax.rem(y + dy, ny) * z_hi + lax.rem(zh + dz, z_hi)

    def chip_peer(t):
        outer = (nx - 1) * z_lo
        dx = jnp.where(t < outer, entry(away[:3], t // z_lo), 0)
        end = jnp.where(zl < z_lo // 2, z_lo - 1 - t % z_lo, t % z_lo)
        to = jnp.where(t < outer, end, lax.rem(zl + t - outer + 1, z_lo))
        return lax.rem(x + dx, nx) * z_lo + to

    mate = (p, chip * 2 + 1 - core)

    fetches = [
        pltpu.make_async_copy(a, b, fetch.at[i])
        for i, (a, b) in enumerate([
            (coords_hbm, coords), (codes_hbm, codes), (tiles_hbm, tiles), (counts_hbm, counts),
            (received_hbm, received), (cotangent_hbm, cotangent), (ids_hbm, group_ids),
            (thresholds_hbm, thresholds),
        ])
    ]
    barrier = pltpu.get_barrier_semaphore()

    def greet(device):
        pl.semaphore_signal(barrier, inc=1, device_id=device, device_id_type=MESH)

    for dz in away[:-1]:
        greet((y * z_hi + lax.rem(zh + dz, z_hi), q))
    for dy in range(1, ny):
        greet((lax.rem(y + dy, ny) * z_hi + zh, q))

    @pl.loop(0, chips - 1)
    def _(t):
        c = chip_peer(t)
        greet((p, c * 2))
        greet((p, c * 2 + 1))

    greet(mate)

    for f in fetches:
        f.start()

    fetches[0].wait()
    fetches[1].wait()
    for k in range(atom_tiles):
        cols = slice(k * T, (k + 1) * T)
        tile = jnp.concatenate(
            [codes[0, :, cols].astype(F32), codes[1, :, cols].astype(F32)], axis=0
        )
        held[k] = tile
        blocks[zh, k] = tile
    dense[...] = held[...].reshape(atom_tiles * V, T).astype(BF16)

    pl.semaphore_wait(barrier, z_hi - 1 + ny - 1 + n_atom - 1)

    def remote(src, dst, s, device, r=None):
        return pltpu.make_async_remote_copy(
            src_ref=src, dst_ref=dst, send_sem=send.at[s], recv_sem=recv.at[s if r is None else r],
            device_id=device, device_id_type=MESH,
        )

    leaving = []

    for dz in away[:-1]:
        to = lax.rem(zh + dz, z_hi)
        remote(dense, dense_recv.at[zh], 15 + dz, (y * z_hi + to, q), 15 + z_hi - dz).start()
        leaving.append((dense, 15 + dz))
    for dy in range(1, ny):
        to = lax.rem(y + dy, ny)
        remote(coords, near.at[y], 0, (to * z_hi + zh, q)).start()

    for l in range(slots):
        for d in range(2):
            near[y, d, l] = coords[d, l]
            places[p, d, l] = coords[d, l]
    if ny > 1:
        wait_bytes(near.at[pl.ds(0, ny - 1)], recv.at[0])
        leaving.append((near.at[pl.ds(0, ny - 1)], 0))

    def build(table, named):
        return jnp.concatenate([table(named(l)) for l in range(slots)], axis=0).astype(BF16)

    for dz in (0, 1, 3, 2):
        z = lax.rem(zh + dz, z_hi)
        if dz:
            wait_bytes(dense_recv.at[z], recv.at[15 + dz])
            blocks[z] = dense_recv[z].astype(F32).reshape(atom_tiles, V, T)
        for dy in range(1, ny):
            to = lax.rem(y + dy, ny)
            codes_send[to, z] = build(lambda k, z=z: blocks[z, k], lambda l, to=to: near[to, 1, l])
            remote(codes_send.at[to, z], codes_recv.at[y * z_hi + z], 2, (to * z_hi + zh, q)).start()
        codes_recv[y * z_hi + z] = build(lambda k, z=z: blocks[z, k], lambda l: coords[1, l])
    fetches[2].wait()
    fetches[3].wait()
    fetches[4].wait()
    rec[...] = received[...].astype(F32)
    if ny > 1:
        wait_bytes(codes_recv.at[pl.ds(0, (ny - 1) * z_hi)], recv.at[2])
        leaving.append((codes_recv.at[pl.ds(0, (ny - 1) * z_hi)], 2))

    @pl.loop(0, n_dof - 1)
    def _(t):
        remote(coords, places.at[p], 1, (dof_peer(t), q)).start()

    leaving.append((places.at[pl.ds(0, n_dof - 1)], 1))

    def hot(flag):
        return jnp.where(flag, 1.0, 0.0).astype(F32)

    live = [hot(l < counts[0, 0]) for l in range(slots)]

    def in_steps(v, axis):
        most = jnp.maximum(jnp.max(jnp.abs(v), axis=axis, keepdims=True), 1e-30)
        steps = jnp.round(v * (STEPS / most)).astype(jnp.int32).astype(jnp.int16)
        return steps, most * (1.0 / STEPS)

    def apply(arrived, picked, put):
        v = arrived[...].astype(F32)
        products = []
        for l in range(slots):
            xl = v[:, l * V : (l + 1) * V, :]
            plain = xl.reshape(rows, T).astype(BF16)
            turned = swap(xl).reshape(rows, T).astype(BF16)
            picked[l, :, :T] = plain
            picked[l, :, T:] = turned
            products.append(nt(plain, tiles[l, 0]) + nt(turned, tiles[l, 1]))
        for r in range(row_tiles):
            acc = products[0] * (live[0] * hot(coords[0, 0] == r))
            for l in range(1, slots):
                acc += products[l] * (live[l] * hot(coords[0, l] == r))
            put(r, acc)

    def rows_of(c):
        return pl.ds(pl.multiple_of(c * chunk, chunk), chunk)

    def to_all(*makes):
        @pl.loop(0, chips - 1)
        def _(t):
            c = chip_peer(t)
            for k in range(2):
                for make in makes:
                    make(c, k).start()

        for make in makes:
            make(chip, 1 - core).start()

    def share_all(share, full, s):
        first = core * n_half + chip * chunk
        place = full.at[first // rows, pl.ds(pl.multiple_of(first % rows, chunk), chunk)]
        to_all(lambda c, k: remote(share, place, s, (p, c * 2 + k)))
        place[...] = share[...]
        leaving.append((sized.at[pl.ds(0, total - chunk)], s))

    def put_part(r, v):
        n = rows // chunk
        steps, scale = in_steps(v.reshape(n, chunk, T), 1)
        part[r * rows : (r + 1) * rows, :] = steps.reshape(rows, T)
        part_scale[r * n : (r + 1) * n] = scale

    def put_back(r, v):
        part_b[r * rows : (r + 1) * rows, :] = v.astype(BF16)

    apply(codes_recv, codes_pick, put_part)
    to_all(
        lambda c, k: remote(part.at[rows_of(k * chips + c)], gather.at[q], 3, (p, c * 2 + k)),
        lambda c, k: remote(
            part_scale.at[k * chips + c], gather_scale.at[q], 4, (p, c * 2 + k)
        ),
    )
    leaving.append((gather.at[pl.ds(0, n_atom - 1)], 3))
    leaving.append((gather_scale.at[pl.ds(0, n_atom - 1)], 4))
    gather[q] = part[rows_of(core * chips + chip), :]
    gather_scale[q] = part_scale[core * chips + chip]
    wait_bytes(gather.at[pl.ds(0, n_atom - 1)], recv.at[3])
    wait_bytes(gather_scale.at[pl.ds(0, n_atom - 1)], recv.at[4])
    acc = jnp.zeros((chunk, T), F32)
    for c in range(n_atom):
        acc += gather[c].astype(jnp.int32).astype(F32) * gather_scale[c]

    first = (core * chips + chip) * chunk
    snaps = pl.ds(pl.multiple_of(first % rows // 2, V), chunk // 2)
    cols = pl.ds(pl.multiple_of(first // rows * T, T), T)
    re, im = rec[0, snaps, cols], rec[1, snaps, cols]
    low = lax.broadcasted_iota(jnp.int32, (V, T), 0) < V // 2
    ordered = []
    for b in range(chunk // (2 * V)):
        a, c = re[b * V : (b + 1) * V], im[b * V : (b + 1) * V]
        ordered.append(jnp.where(low, a, pltpu.roll(c, V // 2, 0)))
        ordered.append(jnp.where(low, pltpu.roll(a, V // 2, 0), c))
    resid_share[...] = (jnp.concatenate(ordered, axis=0) - acc).astype(BF16)
    share_all(resid_share, resid, 5)
    wait_bytes(sized.at[pl.ds(0, total - chunk)], recv.at[5])

    def row_block(ref, l):
        return ref[coords[0, l]]

    corr = []
    for l in range(slots):
        plain = row_block(resid, l)
        turned = swap(plain.astype(F32).reshape(n_dof, V, T)).reshape(rows, T).astype(BF16)
        g = (nn(plain, tiles[l, 0]) - nn(turned, tiles[l, 1])) * live[l]
        corr.append(g.reshape(n_dof, V, T))
    corr_send[...], scale_send[...] = in_steps(jnp.concatenate(corr, axis=1), 1)

    @pl.loop(0, n_dof - 1)
    def _(t):
        peer = dof_peer(t)
        remote(corr_send.at[peer], corr_recv.at[p], 6, (peer, q)).start()
        remote(scale_send.at[peer], scale_recv.at[p], 12, (peer, q)).start()

    leaving.append((corr_recv.at[pl.ds(0, n_dof - 1)], 6))
    leaving.append((scale_recv.at[pl.ds(0, n_dof - 1)], 12))
    corr_recv[p] = corr_send[p]
    scale_recv[p] = scale_send[p]
    fetches[5].wait()
    fetches[6].wait()
    fetches[7].wait()
    wait_bytes(places.at[pl.ds(0, n_dof - 1)], recv.at[1])
    wait_bytes(corr_recv.at[pl.ds(0, n_dof - 1)], recv.at[6])
    wait_bytes(scale_recv.at[pl.ds(0, n_dof - 1)], recv.at[12])

    def add_tiles(peer, acc):
        tiles_in = corr_recv[peer].astype(jnp.int32).astype(F32) * scale_recv[peer]
        for l in range(slots):
            at = jnp.full((V, T), places[peer, 1, l], jnp.int32)
            v = tiles_in[l * V : (l + 1) * V]
            acc = tuple(a + jnp.where(at == k, v, 0.0) for k, a in enumerate(acc))
        return acc

    zero = jnp.zeros((V, T), F32)
    sums = lax.fori_loop(0, n_dof, add_tiles, (zero,) * atom_tiles)

    thr = [zero] * groups
    for k in range(atom_tiles):
        cols = slice(k * T, (k + 1) * T)
        field = held[k] + sums[k]
        theta = jnp.full((V, T), thresholds[group_ids[k]], F32)
        cot = jnp.concatenate(
            [cotangent[0, :, cols].astype(F32), cotangent[1, :, cols].astype(F32)], axis=0
        )
        square = field * field
        magnitude = jnp.sqrt(square + pltpu.roll(square, V // 2, 0) + 1e-06)
        most = jnp.maximum(magnitude, theta)
        factor = jnp.maximum(magnitude - theta, 0.0) / most
        shrunk = (field * factor).astype(BF16)
        next_kept[0, :, cols] = shrunk[: V // 2]
        next_kept[1, :, cols] = shrunk[V // 2 :]
        product = cot * field
        pulled = (product + pltpu.roll(product, V // 2, 0)) / most
        above = jnp.where(magnitude > theta, 1.0, jnp.where(magnitude == theta, 0.5, 0.0))
        pulled = pulled * above
        grad = cot * factor + field * (pulled * (1.0 - factor) / magnitude)
        shares[k] = grad.astype(BF16).astype(F32)
        own = jnp.full((V, T), group_ids[k], jnp.int32)
        thr = [t - jnp.where(own == g, pulled, 0.0) for g, t in enumerate(thr)]

    stores = [pltpu.make_async_copy(next_kept, next_out, fetch.at[1])]
    stores[0].start()

    @pl.loop(0, n_dof - 1)
    def _(t):
        peer = dof_peer(t)
        grad_send[peer] = build(lambda k: shares[k], lambda l: places[peer, 1, l])
        remote(grad_send.at[peer], grad_recv.at[p], 7, (peer, q)).start()

    leaving.append((grad_recv.at[pl.ds(0, n_dof - 1)], 7))
    grad_recv[p] = build(lambda k: shares[k], lambda l: coords[1, l])

    lanes = lax.broadcasted_iota(jnp.int32, (1, T), 1)
    row = jnp.zeros((1, T), F32)
    for g in range(groups):
        row = jnp.where(lanes == g, 0.5 * jnp.sum(thr[g]), row)
    thr_part[...] = row

    @pl.loop(0, n_dof - 1)
    def _(t):
        remote(thr_part, thr_dof.at[p], 8, (dof_peer(t), q)).start()

    leaving.append((thr_dof.at[pl.ds(0, n_dof - 1)], 8))
    thr_dof[p] = thr_part[...]
    wait_bytes(grad_recv.at[pl.ds(0, n_dof - 1)], recv.at[7])

    apply(grad_recv, grad_pick, put_back)
    to_all(
        lambda c, k: remote(
            part_b.at[rows_of(k * chips + c)], gather_b.at[q], 9, (p, c * 2 + k)
        )
    )
    leaving.append((gather_b.at[pl.ds(0, n_atom - 1)], 9))
    gather_b[q] = part_b[rows_of(core * chips + chip), :]
    for l in range(slots):
        lefts[l] = tn(row_block(resid, l), grad_pick[l])
    wait_bytes(gather_b.at[pl.ds(0, n_atom - 1)], recv.at[9])
    acc = gather_b[0].astype(F32)
    for c in range(1, n_atom):
        acc += gather_b[c].astype(F32)
    back_share[...] = acc.astype(BF16)
    share_all(back_share, back, 10)

    wait_bytes(thr_dof.at[pl.ds(0, n_dof - 1)], recv.at[8])
    row = thr_dof[0]
    for i in range(1, n_dof):
        row += thr_dof[i]
    thr_sum[...] = row
    to_all(lambda c, k: remote(thr_sum, thr_atom.at[q], 11, (p, c * 2 + k)))
    leaving.append((thr_atom.at[pl.ds(0, n_atom - 1)], 11))
    thr_atom[q] = row

    wait_bytes(sized.at[pl.ds(0, total - chunk)], recv.at[10])
    for l in range(slots):
        right = tn(row_block(back, l), codes_pick[l])
        g = ((lefts[l] - right) * live[l]).astype(BF16)
        grads_kept[l, 0] = g[:, :T]
        grads_kept[l, 1] = g[:, T:]
        stores.append(pltpu.make_async_copy(grads_kept.at[l], grads_out.at[l], store.at[l]))
        stores[-1].start()

    wait_bytes(thr_atom.at[pl.ds(0, n_atom - 1)], recv.at[11])
    row = thr_atom[0]
    for c in range(1, n_atom):
        row += thr_atom[c]
    for g in range(groups):
        thr_out[g] = jnp.sum(jnp.where(lanes == g, row, 0.0))

    for copy in stores:
        copy.wait()
    for ref, s in leaving:
        wait_bytes(ref, send.at[s])


def hand_over(a, b, c, a_out, b_out, c_out, a_kept, b_kept, c_kept, sem):
    n = b.shape[0]
    parts = [(b.at[l], b_kept.at[l], b_out.at[l]) for l in range(n)]
    parts += [(a, a_kept, a_out), (c, c_kept, c_out)]
    loads = [pltpu.make_async_copy(x, k, sem.at[0, i]) for i, (x, k, _) in enumerate(parts)]
    stores = [pltpu.make_async_copy(k, y, sem.at[1, i]) for i, (_, k, y) in enumerate(parts)]
    for copy in loads:
        copy.start()
    for load, copy in zip(loads, stores):
        load.wait()
        copy.start()
    for copy in stores:
        copy.wait()


def local(n_dof, n_atom, received, codes, tiles, coords, counts, group_ids, thresholds, cotangent):
    slots = tiles.shape[2]
    row_tiles = received.shape[2] // T
    atom_tiles = codes.shape[2] // T
    groups = thresholds.shape[0]
    rows = V * n_dof
    total = row_tiles * rows
    chunk = total // n_atom
    z_hi = 4
    hbm = pl.BlockSpec(memory_space=pltpu.HBM)

    out = pl.pallas_call(
        functools.partial(kernel, n_dof, n_atom, slots, row_tiles, atom_tiles, groups),
        out_shape=(
            jax.ShapeDtypeStruct(codes.shape, BF16),
            jax.ShapeDtypeStruct(tiles.shape[2:], BF16),
            jax.ShapeDtypeStruct((groups,), F32),
        ),
        in_specs=[hbm] * 8,
        out_specs=(hbm, hbm, pl.BlockSpec(memory_space=pltpu.SMEM)),
        scratch_shapes=[
            pltpu.VMEM(received.shape, BF16),
            pltpu.VMEM(codes.shape, BF16),
            pltpu.VMEM(tiles.shape[2:], BF16),
            pltpu.VMEM(codes.shape, BF16),
            pltpu.SMEM((2, slots), jnp.int32),
            pltpu.SMEM(counts.shape, jnp.int32),
            pltpu.SMEM(group_ids.shape, jnp.int32),
            pltpu.SMEM(thresholds.shape, F32),
            pltpu.SMEM((n_dof // z_hi, 2, slots), jnp.int32),
            pltpu.SMEM((n_dof, 2, slots), jnp.int32),
            pltpu.VMEM((atom_tiles, V, T), F32),
            pltpu.VMEM((atom_tiles, V, T), F32),
            pltpu.VMEM(received.shape, F32),
            pltpu.VMEM(codes.shape, BF16),
            pltpu.VMEM(tiles.shape[2:], BF16),
            pltpu.VMEM((atom_tiles * V, T), BF16),
            pltpu.VMEM((z_hi, atom_tiles * V, T), BF16),
            pltpu.VMEM((z_hi, atom_tiles, V, T), F32),
            pltpu.VMEM((n_dof // z_hi, z_hi, slots * V, T), BF16),
            pltpu.VMEM((n_dof, slots * V, T), BF16),
            pltpu.VMEM((n_dof, slots * V, T), jnp.int16),
            pltpu.VMEM((n_dof, slots * V, T), jnp.int16),
            pltpu.VMEM((n_dof, 1, T), F32),
            pltpu.VMEM((n_dof, 1, T), F32),
            pltpu.VMEM((n_dof, slots * V, T), BF16),
            pltpu.VMEM((n_dof, slots * V, T), BF16),
            pltpu.VMEM((slots, rows, 2 * T), BF16),
            pltpu.VMEM((slots, rows, 2 * T), BF16),
            pltpu.VMEM((total, T), jnp.int16),
            pltpu.VMEM((n_atom, 1, T), F32),
            pltpu.VMEM((n_atom, chunk, T), jnp.int16),
            pltpu.VMEM((n_atom, 1, T), F32),
            pltpu.VMEM((row_tiles, rows, T), BF16),
            pltpu.VMEM((chunk, T), BF16),
            pltpu.VMEM((total, T), BF16),
            pltpu.VMEM((n_atom, chunk, T), BF16),
            pltpu.VMEM((row_tiles, rows, T), BF16),
            pltpu.VMEM((chunk, T), BF16),
            pltpu.VMEM((slots, T, 2 * T), F32),
            pltpu.VMEM((total, T), BF16),
            pltpu.VMEM((1, T), F32),
            pltpu.VMEM((n_dof, 1, T), F32),
            pltpu.VMEM((1, T), F32),
            pltpu.VMEM((n_atom, 1, T), F32),
            pltpu.SemaphoreType.DMA((19,)),
            pltpu.SemaphoreType.DMA((19,)),
            pltpu.SemaphoreType.DMA((8,)),
            pltpu.SemaphoreType.DMA((slots,)),
        ],
        compiler_params=pltpu.CompilerParams(
            collective_id=0, has_side_effects=True, vmem_limit_bytes=62 * 1024 * 1024
        ),
    )(received, codes, tiles[0, 0], coords[0, 0].T, counts, group_ids, thresholds, cotangent)
    codes_next, tile_grads, threshold_grads = pl.pallas_call(
        hand_over,
        out_shape=tuple(jax.ShapeDtypeStruct(o.shape, o.dtype) for o in out),
        in_specs=[hbm] * 3,
        out_specs=(hbm,) * 3,
        scratch_shapes=[
            pltpu.VMEM(codes.shape, BF16),
            pltpu.VMEM(tiles.shape[2:], BF16),
            pltpu.SMEM((groups,), F32),
            pltpu.SemaphoreType.DMA((2, slots + 2)),
        ],
        compiler_params=pltpu.CompilerParams(vmem_limit_bytes=62 * 1024 * 1024),
    )(*out)
    return codes_next, tile_grads[None, None], threshold_grads


def solution(mesh):
    placed = (
        P(None, None, "dof"),
        P(None, "dof", "atom"),
        P("dof", "atom", None, None, None, None),
        P("dof", "atom", None, None),
        P("dof", "atom"),
        P("atom"),
        P(),
        P(None, "dof", "atom"),
    )
    return jax.shard_map(
        functools.partial(local, mesh.shape["dof"], mesh.shape["atom"]),
        mesh=mesh,
        in_specs=placed,
        out_specs=(P(None, "dof", "atom"), P("dof", "atom", None, None, None, None), P()),
        check_vma=False,
    )
```

```python
import functools

import jax
import jax.numpy as jnp
from jax import lax
from jax.experimental import pallas as pl
from jax.experimental.pallas import tpu as pltpu
from jax.sharding import PartitionSpec as P

MESH = pl.DeviceIdType.MESH
F32 = jnp.float32
BF16 = jnp.bfloat16
STEPS = 32000.0
T = 128
V = 8


def swap(x):
    turned = pltpu.roll(x, V // 2, 1)
    rows = lax.broadcasted_iota(jnp.int32, x.shape, 1)
    return jnp.where(rows < V // 2, -turned, turned)


def nt(a, b):
    return lax.dot_general(a, b, (((1,), (1,)), ((), ())), preferred_element_type=F32)


def nn(a, b):
    return lax.dot_general(a, b, (((1,), (0,)), ((), ())), preferred_element_type=F32)


def tn(a, b):
    return lax.dot_general(a, b, (((0,), (0,)), ((), ())), preferred_element_type=F32)


def wait_bytes(ref, sem):
    pltpu.make_async_copy(ref, ref, sem).wait()


def entry(values, t):
    out = values[-1]
    for i in reversed(range(len(values) - 1)):
        out = jnp.where(t == i, values[i], out)
    return out


def kernel(
    n_dof, n_atom, slots, row_tiles, atom_tiles, groups,
    received_hbm, codes_hbm, tiles_hbm, coords_hbm, counts_hbm, ids_hbm, thresholds_hbm, cotangent_hbm,
    next_out, grads_out, thr_out,
    received, codes, tiles, cotangent, coords, counts, group_ids, thresholds,
    near, places, held, shares, rec, next_kept, grads_kept,
    dense, dense_recv, blocks, codes_send, codes_recv,
    corr_send, corr_recv, scale_send, scale_recv, grad_send, grad_recv, codes_pick, grad_pick,
    part, part_scale, gather, gather_scale, resid, resid_share,
    part_b, gather_b, back, back_share, lefts, sized,
    thr_part, thr_dof, thr_sum, thr_atom,
    send, recv, fetch, store,
):
    p = lax.axis_index("dof")
    q = lax.axis_index("atom")
    z_hi, z_lo = 4, 4
    ny, nx = n_dof // z_hi, n_atom // (2 * z_lo)
    chips = n_atom // 2
    chip, core = q // 2, q % 2
    y, zh = p // z_hi, p % z_hi
    x, zl = chip // z_lo, chip % z_lo
    rows = V * n_dof
    total = row_tiles * rows
    chunk = total // n_atom
    n_half = total // 2
    away = (2, 1, 3, 0)

    def dof_peer(t):
        dz, dy = entry(away, t // ny), (entry(away, t % ny) if ny > 1 else 0)
        return lax.rem(y + dy, ny) * z_hi + lax.rem(zh + dz, z_hi)

    def chip_peer(t):
        outer = (nx - 1) * z_lo
        dx = jnp.where(t < outer, entry(away[:3], t // z_lo), 0)
        end = jnp.where(zl < z_lo // 2, z_lo - 1 - t % z_lo, t % z_lo)
        to = jnp.where(t < outer, end, lax.rem(zl + t - outer + 1, z_lo))
        return lax.rem(x + dx, nx) * z_lo + to

    mate = (p, chip * 2 + 1 - core)

    fetches = [
        pltpu.make_async_copy(a, b, fetch.at[i])
        for i, (a, b) in enumerate([
            (coords_hbm, coords), (codes_hbm, codes), (tiles_hbm, tiles), (counts_hbm, counts),
            (received_hbm, received), (cotangent_hbm, cotangent), (ids_hbm, group_ids),
            (thresholds_hbm, thresholds),
        ])
    ]
    barrier = pltpu.get_barrier_semaphore()

    def greet(device):
        pl.semaphore_signal(barrier, inc=1, device_id=device, device_id_type=MESH)

    for dz in away[:-1]:
        greet((y * z_hi + lax.rem(zh + dz, z_hi), q))
    for dy in range(1, ny):
        greet((lax.rem(y + dy, ny) * z_hi + zh, q))

    @pl.loop(0, chips - 1)
    def _(t):
        c = chip_peer(t)
        greet((p, c * 2))
        greet((p, c * 2 + 1))

    greet(mate)

    for f in fetches:
        f.start()

    fetches[0].wait()
    fetches[1].wait()
    for k in range(atom_tiles):
        cols = slice(k * T, (k + 1) * T)
        tile = jnp.concatenate(
            [codes[0, :, cols].astype(F32), codes[1, :, cols].astype(F32)], axis=0
        )
        held[k] = tile
        blocks[zh, k] = tile
    dense[...] = held[...].reshape(atom_tiles * V, T).astype(BF16)

    pl.semaphore_wait(barrier, z_hi - 1 + ny - 1 + n_atom - 1)

    def remote(src, dst, s, device, r=None):
        return pltpu.make_async_remote_copy(
            src_ref=src, dst_ref=dst, send_sem=send.at[s], recv_sem=recv.at[s if r is None else r],
            device_id=device, device_id_type=MESH,
        )

    leaving = []

    for dz in away[:-1]:
        to = lax.rem(zh + dz, z_hi)
        remote(dense, dense_recv.at[zh], 15 + dz, (y * z_hi + to, q), 15 + z_hi - dz).start()
        leaving.append((dense, 15 + dz))
    for dy in range(1, ny):
        to = lax.rem(y + dy, ny)
        remote(coords, near.at[y], 0, (to * z_hi + zh, q)).start()

    for l in range(slots):
        for d in range(2):
            near[y, d, l] = coords[d, l]
            places[p, d, l] = coords[d, l]
    if ny > 1:
        wait_bytes(near.at[pl.ds(0, ny - 1)], recv.at[0])
        leaving.append((near.at[pl.ds(0, ny - 1)], 0))

    def build(table, named):
        return jnp.concatenate([table(named(l)) for l in range(slots)], axis=0).astype(BF16)

    for dz in (0, 1, 3, 2):
        z = lax.rem(zh + dz, z_hi)
        if dz:
            wait_bytes(dense_recv.at[z], recv.at[15 + dz])
            blocks[z] = dense_recv[z].astype(F32).reshape(atom_tiles, V, T)
        for dy in range(1, ny):
            to = lax.rem(y + dy, ny)
            codes_send[to, z] = build(lambda k, z=z: blocks[z, k], lambda l, to=to: near[to, 1, l])
            remote(codes_send.at[to, z], codes_recv.at[y * z_hi + z], 2, (to * z_hi + zh, q)).start()
        codes_recv[y * z_hi + z] = build(lambda k, z=z: blocks[z, k], lambda l: coords[1, l])
    fetches[2].wait()
    fetches[3].wait()
    fetches[4].wait()
    rec[...] = received[...].astype(F32)
    if ny > 1:
        wait_bytes(codes_recv.at[pl.ds(0, (ny - 1) * z_hi)], recv.at[2])
        leaving.append((codes_recv.at[pl.ds(0, (ny - 1) * z_hi)], 2))

    @pl.loop(0, n_dof - 1)
    def _(t):
        remote(coords, places.at[p], 1, (dof_peer(t), q)).start()

    leaving.append((places.at[pl.ds(0, n_dof - 1)], 1))

    def hot(flag):
        return jnp.where(flag, 1.0, 0.0).astype(F32)

    live = [hot(l < counts[0, 0]) for l in range(slots)]

    def in_steps(v, axis):
        most = jnp.maximum(jnp.max(jnp.abs(v), axis=axis, keepdims=True), 1e-30)
        steps = jnp.round(v * (STEPS / most)).astype(jnp.int32).astype(jnp.int16)
        return steps, most * (1.0 / STEPS)

    def apply(arrived, picked, put):
        v = arrived[...].astype(F32)
        products = []
        for l in range(slots):
            xl = v[:, l * V : (l + 1) * V, :]
            plain = xl.reshape(rows, T).astype(BF16)
            turned = swap(xl).reshape(rows, T).astype(BF16)
            picked[l, :, :T] = plain
            picked[l, :, T:] = turned
            products.append(nt(plain, tiles[l, 0]) + nt(turned, tiles[l, 1]))
        for r in range(row_tiles):
            acc = products[0] * (live[0] * hot(coords[0, 0] == r))
            for l in range(1, slots):
                acc += products[l] * (live[l] * hot(coords[0, l] == r))
            put(r, acc)

    def rows_of(c):
        return pl.ds(pl.multiple_of(c * chunk, chunk), chunk)

    def to_all(*makes):
        @pl.loop(0, chips - 1)
        def _(t):
            c = chip_peer(t)
            for k in range(2):
                for make in makes:
                    make(c, k).start()

        for make in makes:
            make(chip, 1 - core).start()

    def share_all(share, full, s):
        first = core * n_half + chip * chunk
        place = full.at[first // rows, pl.ds(pl.multiple_of(first % rows, chunk), chunk)]
        to_all(lambda c, k: remote(share, place, s, (p, c * 2 + k)))
        place[...] = share[...]
        leaving.append((sized.at[pl.ds(0, total - chunk)], s))

    def put_part(r, v):
        n = rows // chunk
        steps, scale = in_steps(v.reshape(n, chunk, T), 1)
        part[r * rows : (r + 1) * rows, :] = steps.reshape(rows, T)
        part_scale[r * n : (r + 1) * n] = scale

    def put_back(r, v):
        part_b[r * rows : (r + 1) * rows, :] = v.astype(BF16)

    apply(codes_recv, codes_pick, put_part)
    to_all(
        lambda c, k: remote(part.at[rows_of(k * chips + c)], gather.at[q], 3, (p, c * 2 + k)),
        lambda c, k: remote(
            part_scale.at[k * chips + c], gather_scale.at[q], 4, (p, c * 2 + k)
        ),
    )
    leaving.append((gather.at[pl.ds(0, n_atom - 1)], 3))
    leaving.append((gather_scale.at[pl.ds(0, n_atom - 1)], 4))
    gather[q] = part[rows_of(core * chips + chip), :]
    gather_scale[q] = part_scale[core * chips + chip]
    wait_bytes(gather.at[pl.ds(0, n_atom - 1)], recv.at[3])
    wait_bytes(gather_scale.at[pl.ds(0, n_atom - 1)], recv.at[4])
    acc = jnp.zeros((chunk, T), F32)
    for c in range(n_atom):
        acc += gather[c].astype(jnp.int32).astype(F32) * gather_scale[c]

    first = (core * chips + chip) * chunk
    snaps = pl.ds(pl.multiple_of(first % rows // 2, V), chunk // 2)
    cols = pl.ds(pl.multiple_of(first // rows * T, T), T)
    re, im = rec[0, snaps, cols], rec[1, snaps, cols]
    low = lax.broadcasted_iota(jnp.int32, (V, T), 0) < V // 2
    ordered = []
    for b in range(chunk // (2 * V)):
        a, c = re[b * V : (b + 1) * V], im[b * V : (b + 1) * V]
        ordered.append(jnp.where(low, a, pltpu.roll(c, V // 2, 0)))
        ordered.append(jnp.where(low, pltpu.roll(a, V // 2, 0), c))
    resid_share[...] = (jnp.concatenate(ordered, axis=0) - acc).astype(BF16)
    share_all(resid_share, resid, 5)
    wait_bytes(sized.at[pl.ds(0, total - chunk)], recv.at[5])

    def row_block(ref, l):
        return ref[coords[0, l]]

    corr = []
    for l in range(slots):
        plain = row_block(resid, l)
        turned = swap(plain.astype(F32).reshape(n_dof, V, T)).reshape(rows, T).astype(BF16)
        g = (nn(plain, tiles[l, 0]) - nn(turned, tiles[l, 1])) * live[l]
        corr.append(g.reshape(n_dof, V, T))
    corr_send[...], scale_send[...] = in_steps(jnp.concatenate(corr, axis=1), 1)

    @pl.loop(0, n_dof - 1)
    def _(t):
        peer = dof_peer(t)
        remote(corr_send.at[peer], corr_recv.at[p], 6, (peer, q)).start()
        remote(scale_send.at[peer], scale_recv.at[p], 12, (peer, q)).start()

    leaving.append((corr_recv.at[pl.ds(0, n_dof - 1)], 6))
    leaving.append((scale_recv.at[pl.ds(0, n_dof - 1)], 12))
    corr_recv[p] = corr_send[p]
    scale_recv[p] = scale_send[p]
    fetches[5].wait()
    fetches[6].wait()
    fetches[7].wait()
    wait_bytes(places.at[pl.ds(0, n_dof - 1)], recv.at[1])
    wait_bytes(corr_recv.at[pl.ds(0, n_dof - 1)], recv.at[6])
    wait_bytes(scale_recv.at[pl.ds(0, n_dof - 1)], recv.at[12])

    def add_tiles(peer, acc):
        tiles_in = corr_recv[peer].astype(jnp.int32).astype(F32) * scale_recv[peer]
        for l in range(slots):
            at = jnp.full((V, T), places[peer, 1, l], jnp.int32)
            v = tiles_in[l * V : (l + 1) * V]
            acc = tuple(a + jnp.where(at == k, v, 0.0) for k, a in enumerate(acc))
        return acc

    zero = jnp.zeros((V, T), F32)
    sums = lax.fori_loop(0, n_dof, add_tiles, (zero,) * atom_tiles)

    thr = [zero] * groups
    for k in range(atom_tiles):
        cols = slice(k * T, (k + 1) * T)
        field = held[k] + sums[k]
        theta = jnp.full((V, T), thresholds[group_ids[k]], F32)
        cot = jnp.concatenate(
            [cotangent[0, :, cols].astype(F32), cotangent[1, :, cols].astype(F32)], axis=0
        )
        square = field * field
        magnitude = jnp.sqrt(square + pltpu.roll(square, V // 2, 0) + 1e-06)
        most = jnp.maximum(magnitude, theta)
        factor = jnp.maximum(magnitude - theta, 0.0) / most
        shrunk = (field * factor).astype(BF16)
        next_kept[0, :, cols] = shrunk[: V // 2]
        next_kept[1, :, cols] = shrunk[V // 2 :]
        product = cot * field
        pulled = (product + pltpu.roll(product, V // 2, 0)) / most
        above = jnp.where(magnitude > theta, 1.0, jnp.where(magnitude == theta, 0.5, 0.0))
        pulled = pulled * above
        grad = cot * factor + field * (pulled * (1.0 - factor) / magnitude)
        shares[k] = grad.astype(BF16).astype(F32)
        own = jnp.full((V, T), group_ids[k], jnp.int32)
        thr = [t - jnp.where(own == g, pulled, 0.0) for g, t in enumerate(thr)]

    stores = [pltpu.make_async_copy(next_kept, next_out, fetch.at[1])]
    stores[0].start()

    @pl.loop(0, n_dof - 1)
    def _(t):
        peer = dof_peer(t)
        grad_send[peer] = build(lambda k: shares[k], lambda l: places[peer, 1, l])
        remote(grad_send.at[peer], grad_recv.at[p], 7, (peer, q)).start()

    leaving.append((grad_recv.at[pl.ds(0, n_dof - 1)], 7))
    grad_recv[p] = build(lambda k: shares[k], lambda l: coords[1, l])

    lanes = lax.broadcasted_iota(jnp.int32, (1, T), 1)
    row = jnp.zeros((1, T), F32)
    for g in range(groups):
        row = jnp.where(lanes == g, 0.5 * jnp.sum(thr[g]), row)
    thr_part[...] = row

    @pl.loop(0, n_dof - 1)
    def _(t):
        remote(thr_part, thr_dof.at[p], 8, (dof_peer(t), q)).start()

    leaving.append((thr_dof.at[pl.ds(0, n_dof - 1)], 8))
    thr_dof[p] = thr_part[...]
    wait_bytes(grad_recv.at[pl.ds(0, n_dof - 1)], recv.at[7])

    apply(grad_recv, grad_pick, put_back)
    to_all(
        lambda c, k: remote(
            part_b.at[rows_of(k * chips + c)], gather_b.at[q], 9, (p, c * 2 + k)
        )
    )
    leaving.append((gather_b.at[pl.ds(0, n_atom - 1)], 9))
    gather_b[q] = part_b[rows_of(core * chips + chip), :]
    wait_bytes(thr_dof.at[pl.ds(0, n_dof - 1)], recv.at[8])
    row = thr_dof[0]
    for i in range(1, n_dof):
        row += thr_dof[i]
    thr_sum[...] = row
    to_all(lambda c, k: remote(thr_sum, thr_atom.at[q], 11, (p, c * 2 + k)))
    leaving.append((thr_atom.at[pl.ds(0, n_atom - 1)], 11))
    thr_atom[q] = row

    for l in range(slots):
        lefts[l] = tn(row_block(resid, l), grad_pick[l])
    wait_bytes(gather_b.at[pl.ds(0, n_atom - 1)], recv.at[9])
    acc = gather_b[0].astype(F32)
    for c in range(1, n_atom):
        acc += gather_b[c].astype(F32)
    back_share[...] = acc.astype(BF16)
    share_all(back_share, back, 10)

    wait_bytes(thr_atom.at[pl.ds(0, n_atom - 1)], recv.at[11])
    row = thr_atom[0]
    for c in range(1, n_atom):
        row += thr_atom[c]
    for g in range(groups):
        thr_out[g] = jnp.sum(jnp.where(lanes == g, row, 0.0))

    wait_bytes(sized.at[pl.ds(0, total - chunk)], recv.at[10])
    for l in range(slots):
        right = tn(row_block(back, l), codes_pick[l])
        g = ((lefts[l] - right) * live[l]).astype(BF16)
        grads_kept[l, 0] = g[:, :T]
        grads_kept[l, 1] = g[:, T:]
        stores.append(pltpu.make_async_copy(grads_kept.at[l], grads_out.at[l], store.at[l]))
        stores[-1].start()

    for copy in stores:
        copy.wait()
    for ref, s in leaving:
        wait_bytes(ref, send.at[s])


def hand_over(a, b, c, a_out, b_out, c_out, a_kept, b_kept, c_kept, sem):
    n = b.shape[0]
    parts = [(b.at[l], b_kept.at[l], b_out.at[l]) for l in range(n)]
    parts += [(a, a_kept, a_out), (c, c_kept, c_out)]
    loads = [pltpu.make_async_copy(x, k, sem.at[0, i]) for i, (x, k, _) in enumerate(parts)]
    stores = [pltpu.make_async_copy(k, y, sem.at[1, i]) for i, (_, k, y) in enumerate(parts)]
    for copy in loads:
        copy.start()
    for load, copy in zip(loads, stores):
        load.wait()
        copy.start()
    for copy in stores:
        copy.wait()


def local(n_dof, n_atom, received, codes, tiles, coords, counts, group_ids, thresholds, cotangent):
    slots = tiles.shape[2]
    row_tiles = received.shape[2] // T
    atom_tiles = codes.shape[2] // T
    groups = thresholds.shape[0]
    rows = V * n_dof
    total = row_tiles * rows
    chunk = total // n_atom
    z_hi = 4
    hbm = pl.BlockSpec(memory_space=pltpu.HBM)

    out = pl.pallas_call(
        functools.partial(kernel, n_dof, n_atom, slots, row_tiles, atom_tiles, groups),
        out_shape=(
            jax.ShapeDtypeStruct(codes.shape, BF16),
            jax.ShapeDtypeStruct(tiles.shape[2:], BF16),
            jax.ShapeDtypeStruct((groups,), F32),
        ),
        in_specs=[hbm] * 8,
        out_specs=(hbm, hbm, pl.BlockSpec(memory_space=pltpu.SMEM)),
        scratch_shapes=[
            pltpu.VMEM(received.shape, BF16),
            pltpu.VMEM(codes.shape, BF16),
            pltpu.VMEM(tiles.shape[2:], BF16),
            pltpu.VMEM(codes.shape, BF16),
            pltpu.SMEM((2, slots), jnp.int32),
            pltpu.SMEM(counts.shape, jnp.int32),
            pltpu.SMEM(group_ids.shape, jnp.int32),
            pltpu.SMEM(thresholds.shape, F32),
            pltpu.SMEM((n_dof // z_hi, 2, slots), jnp.int32),
            pltpu.SMEM((n_dof, 2, slots), jnp.int32),
            pltpu.VMEM((atom_tiles, V, T), F32),
            pltpu.VMEM((atom_tiles, V, T), F32),
            pltpu.VMEM(received.shape, F32),
            pltpu.VMEM(codes.shape, BF16),
            pltpu.VMEM(tiles.shape[2:], BF16),
            pltpu.VMEM((atom_tiles * V, T), BF16),
            pltpu.VMEM((z_hi, atom_tiles * V, T), BF16),
            pltpu.VMEM((z_hi, atom_tiles, V, T), F32),
            pltpu.VMEM((n_dof // z_hi, z_hi, slots * V, T), BF16),
            pltpu.VMEM((n_dof, slots * V, T), BF16),
            pltpu.VMEM((n_dof, slots * V, T), jnp.int16),
            pltpu.VMEM((n_dof, slots * V, T), jnp.int16),
            pltpu.VMEM((n_dof, 1, T), F32),
            pltpu.VMEM((n_dof, 1, T), F32),
            pltpu.VMEM((n_dof, slots * V, T), BF16),
            pltpu.VMEM((n_dof, slots * V, T), BF16),
            pltpu.VMEM((slots, rows, 2 * T), BF16),
            pltpu.VMEM((slots, rows, 2 * T), BF16),
            pltpu.VMEM((total, T), jnp.int16),
            pltpu.VMEM((n_atom, 1, T), F32),
            pltpu.VMEM((n_atom, chunk, T), jnp.int16),
            pltpu.VMEM((n_atom, 1, T), F32),
            pltpu.VMEM((row_tiles, rows, T), BF16),
            pltpu.VMEM((chunk, T), BF16),
            pltpu.VMEM((total, T), BF16),
            pltpu.VMEM((n_atom, chunk, T), BF16),
            pltpu.VMEM((row_tiles, rows, T), BF16),
            pltpu.VMEM((chunk, T), BF16),
            pltpu.VMEM((slots, T, 2 * T), F32),
            pltpu.VMEM((total, T), BF16),
            pltpu.VMEM((1, T), F32),
            pltpu.VMEM((n_dof, 1, T), F32),
            pltpu.VMEM((1, T), F32),
            pltpu.VMEM((n_atom, 1, T), F32),
            pltpu.SemaphoreType.DMA((19,)),
            pltpu.SemaphoreType.DMA((19,)),
            pltpu.SemaphoreType.DMA((8,)),
            pltpu.SemaphoreType.DMA((slots,)),
        ],
        compiler_params=pltpu.CompilerParams(
            collective_id=0, has_side_effects=True, vmem_limit_bytes=62 * 1024 * 1024
        ),
    )(received, codes, tiles[0, 0], coords[0, 0].T, counts, group_ids, thresholds, cotangent)
    codes_next, tile_grads, threshold_grads = pl.pallas_call(
        hand_over,
        out_shape=tuple(jax.ShapeDtypeStruct(o.shape, o.dtype) for o in out),
        in_specs=[hbm] * 3,
        out_specs=(hbm,) * 3,
        scratch_shapes=[
            pltpu.VMEM(codes.shape, BF16),
            pltpu.VMEM(tiles.shape[2:], BF16),
            pltpu.SMEM((groups,), F32),
            pltpu.SemaphoreType.DMA((2, slots + 2)),
        ],
        compiler_params=pltpu.CompilerParams(vmem_limit_bytes=62 * 1024 * 1024),
    )(*out)
    return codes_next, tile_grads[None, None], threshold_grads


def solution(mesh):
    placed = (
        P(None, None, "dof"),
        P(None, "dof", "atom"),
        P("dof", "atom", None, None, None, None),
        P("dof", "atom", None, None),
        P("dof", "atom"),
        P("atom"),
        P(),
        P(None, "dof", "atom"),
    )
    return jax.shard_map(
        functools.partial(local, mesh.shape["dof"], mesh.shape["atom"]),
        mesh=mesh,
        in_specs=placed,
        out_specs=(P(None, "dof", "atom"), P("dof", "atom", None, None, None, None), P()),
        check_vma=False,
    )
```
